128 devices in a mesh: lat: 8 (over x, z_hi), lon: 16 (over z_lo, y, core).
Axes of the slice: x: 4, y: 4, z: 4 (z_hi: 2, z_lo: 2; z = z_hi * 2 + z_lo), core: 2. Of those that a mesh axis runs over, the one named last changes fastest.
Arguments:
- tokens: bfloat16 [1, 96, 384, 512], P(None, 'lat', 'lon'), may hold values from -6 to 6
- qkv_first: bfloat16 [1536, 512], replicated, may hold values from -1 to 1, as said below
- out_first: bfloat16 [512, 512], replicated, may hold values from -0.25 to 0.25
- qkv_second: bfloat16 [1536, 512], replicated, may hold values from -1 to 1, as said below
- out_second: bfloat16 [512, 512], replicated, may hold values from -0.25 to 0.25
- merge_weight: bfloat16 [1024, 2048], replicated, may hold values from -0.125 to 0.125
- qkv_third: bfloat16 [3072, 1024], replicated, may hold values from -1 to 1, as said below
- out_third: bfloat16 [1024, 1024], replicated, may hold values from -0.1875 to 0.1875
- cotangent: bfloat16 [1, 48, 192, 1024], P(None, 'lat', 'lon'), may hold values from -6 to 6
Outputs:
- latent: bfloat16 [1, 48, 192, 1024], P(None, 'lat', 'lon')
- tokens_grad: bfloat16 [1, 96, 384, 512], P(None, 'lat', 'lon')
- qkv_first_grad: float32 [1536, 512], P(('lat', 'lon'))
- out_first_grad: float32 [512, 512], P(('lat', 'lon'))
- qkv_second_grad: float32 [1536, 512], P(('lat', 'lon'))
- out_second_grad: float32 [512, 512], P(('lat', 'lon'))
- merge_grad: float32 [1024, 2048], P(('lat', 'lon'))
- qkv_third_grad: float32 [3072, 1024], P(('lat', 'lon'))
- out_third_grad: float32 [1024, 1024], P(('lat', 'lon'))
The draws below stay inside these ranges and needn't reach their ends.
Inputs may be any that keep to these rules, and one draw needn't show every extreme that they name: `qkv_first`: a query, key and value projection, query and key rows first. `qkv_second`: a query, key and value projection, query and key rows first. `qkv_third`: a query, key and value projection, query and key rows first.
All inputs are finite; a program needn't handle non-finite values.
Results may differ from the reference program's by a relative error of at most 0.04.
Values may be sent and summed in bfloat16 or wider, within the bound.
No kernel may reach another device: no remote copies, remote signals or barrier semaphores. Data moves between devices by JAX's collectives and lax.ppermute only.
A program may use at most 192 MiB of HBM per device.

```python
import jax
import jax.numpy as jnp
from jax import lax

C = 512
C2 = 1024
HDIM = 64
LEV = 1
WA = 6
WO = 12
LAT = 96
LON = 384
LAT2 = 48
LON2 = 192


def projection_draw(key, channels, strength_top):
    first_key, second_key, third_key = jax.random.split(key, 3)
    base = jax.random.normal(first_key, (3 * channels, channels), jnp.float32) * channels ** (-0.5)
    shared = jax.random.normal(second_key, (channels, channels), jnp.float32) * channels ** (-0.5)
    head_count = channels // HDIM
    strength = strength_top * jnp.exp(-1.8 * jax.random.uniform(third_key, (head_count,), jnp.float32))
    scaled = jnp.repeat(strength, HDIM)[:, None] * shared
    extra = jnp.concatenate([scaled, scaled, jnp.zeros((channels, channels), jnp.float32)], axis=0)
    return jnp.clip(base + extra, -1.0, 1.0).astype(jnp.bfloat16)


def draw_qkv_first(key, part):
    key = jax.random.fold_in(key, 5)
    strength_top = 0.0
    return projection_draw(key, C, strength_top)


def draw_qkv_second(key, part):
    key = jax.random.fold_in(key, 7)
    strength_top = 0.0
    return projection_draw(key, C, strength_top)


def draw_qkv_third(key, part):
    key = jax.random.fold_in(key, 9)
    strength_top = 0.0
    return projection_draw(key, C2, strength_top)


def spiked(values, key, source, target, blocks, factor):
    owner, partner = [(jnp.arange(values.shape[dim]) // (values.shape[dim] // blocks)).reshape([-1 if axis == dim else 1 for axis in range(values.ndim)]) for dim in (source, target)]
    chosen = jax.random.permutation(key, blocks)[partner]
    strong = (owner == chosen) | (owner == (partner + blocks // 2) % blocks)
    return jnp.where(strong, factor * values, values)


def shard_levels(own_key, dims, cuts, low, largest):
    def one(dim, parts):
        heights = jax.random.uniform(jax.random.fold_in(jax.random.fold_in(own_key, 6), dim), (parts,), jnp.float32, low / len(cuts), largest / len(cuts))
        return jnp.repeat(jnp.exp(heights), dims[dim] // parts).reshape((-1,) + (1,) * (len(dims) - dim - 1))

    factor_of = one(*cuts[0])
    for cut in cuts[1:]:
        factor_of = factor_of * one(*cut)
    return factor_of


def bell_draw(key, shape, spread, most, shards=(), kind=jnp.bfloat16):
    array = spread * jax.random.normal(key, shape, jnp.float32)
    if shards:
        array = array * shard_levels(key, shape, shards, -0.22, 0.18)
    return jnp.clip(array, -most, most).astype(kind)


def gaussian_with(own_key, extent, width, reach, cuts, heavy, held_as=jnp.bfloat16):
    values = width * jax.random.normal(own_key, extent, jnp.float32)
    if cuts:
        values = values * shard_levels(own_key, extent, cuts, -0.22, 0.18)
    return jnp.clip(spiked(values, jax.random.fold_in(own_key, 3), *heavy), -reach, reach).astype(held_as)


def setup_inputs(seed: int = 0) -> dict:
    streams_of = jax.random.split(jax.random.key(seed), 10)
    return {
        "tokens": bell_draw(streams_of[0], (LEV, LAT, LON, C), 1.0, 6.0, ((1, 8), (2, 16))),
        "qkv_first": draw_qkv_first(jax.random.fold_in(streams_of[9], 71), 0),
        "out_first": bell_draw(streams_of[2], (C, C), C ** -0.5, 0.25),
        "qkv_second": draw_qkv_second(jax.random.fold_in(streams_of[9], 71), 0),
        "out_second": bell_draw(streams_of[4], (C, C), C ** -0.5, 0.25),
        "merge_weight": bell_draw(streams_of[5], (C2, 4 * C), (4 * C) ** -0.5, 0.125),
        "qkv_third": draw_qkv_third(jax.random.fold_in(streams_of[9], 71), 0),
        "out_third": bell_draw(streams_of[7], (C2, C2), C2 ** -0.5, 0.1875),
        "cotangent": gaussian_with(streams_of[8], (LEV, LAT2, LON2, C2), 1.0, 6.0, ((1, 8), (2, 16)), (2, 3, 16, 2.0)),
    }


EPSILON = 1e-05

def normalize(field):
    values = field.astype(jnp.float32)
    average = lax.optimization_barrier(jnp.mean(values, axis=-1, keepdims=True))
    centered = values - average
    variance = lax.optimization_barrier(jnp.mean(centered * centered, axis=-1, keepdims=True))
    return (centered * lax.rsqrt(variance + EPSILON)).astype(jnp.bfloat16)

def project(rows, matrix):
    return lax.dot_general(rows, matrix, (((1,), (1,)), ((), ())), preferred_element_type=jnp.float32)

def grad_weight(cotan, rows):
    return lax.dot_general(cotan, rows, (((0,), (0,)), ((), ())), preferred_element_type=jnp.float32)

def pull_back(cotan, matrix):
    return jnp.dot(cotan, matrix, preferred_element_type=jnp.float32).astype(jnp.bfloat16)

def combine(first_term, second_term):
    return (first_term.astype(jnp.float32) + second_term.astype(jnp.float32)).astype(jnp.bfloat16)

def windows(field, lat_win, lon_win):
    levels, lat_rows, lon_cols, channels = field.shape
    blocked = field.reshape(levels, lat_rows // lat_win, lat_win, lon_cols // lon_win, lon_win, channels)
    blocked = blocked.transpose(1, 3, 0, 2, 4, 5)
    return blocked.reshape(lat_rows // lat_win * (lon_cols // lon_win), levels * lat_win * lon_win, channels)

def unwindows(blocks, grid_shape, lat_win, lon_win):
    levels, lat_rows, lon_cols, channels = grid_shape
    blocked = blocks.reshape(lat_rows // lat_win, lon_cols // lon_win, levels, lat_win, lon_win, channels)
    blocked = blocked.transpose(2, 0, 3, 1, 4, 5)
    return blocked.reshape(levels, lat_rows, lon_cols, channels)

def merge_patches(field):
    levels, lat_rows, lon_cols, channels = field.shape
    blocked = field.reshape(levels, lat_rows // 2, 2, lon_cols // 2, 2, channels).transpose(0, 1, 3, 4, 2, 5)
    return blocked.reshape(levels, lat_rows // 2, lon_cols // 2, 4 * channels)

def split_patches(field):
    levels, lat_half, lon_half, four_channels = field.shape
    blocked = field.reshape(levels, lat_half, lon_half, 2, 2, four_channels // 4).transpose(0, 1, 4, 2, 3, 5)
    return blocked.reshape(levels, 2 * lat_half, 2 * lon_half, four_channels // 4)

def region_bias(rows_start, lat_total, grid_shape, lat_win, lon_win):
    levels, lat_rows, lon_cols, channels = grid_shape
    row_index = rows_start + jnp.arange(lat_rows, dtype=jnp.int32)
    region = (row_index >= lat_total - lat_win).astype(jnp.float32) + (row_index >= lat_total - lat_win // 2).astype(jnp.float32)
    region_grid = jnp.broadcast_to(region[None, :, None, None], (levels, lat_rows, lon_cols, 1))
    region_tags = windows(region_grid, lat_win, lon_win)[:, :, 0]
    same = region_tags[:, :, None] == region_tags[:, None, :]
    return jnp.where(same, jnp.float32(0.0), jnp.float32(-1e+30)).astype(jnp.float32)

def attend(packed, mask_bias):
    window_count, window_size, triple_width = packed.shape
    channels = triple_width // 3
    head_count = channels // HDIM
    unpacked = packed.astype(jnp.float32).reshape(window_count, window_size, 3, head_count, HDIM)
    scores = jnp.einsum('wqhd,wkhd->whqk', unpacked[:, :, 0], unpacked[:, :, 1], precision=lax.Precision.HIGHEST)
    scores = scores * HDIM ** (-0.5) + mask_bias[:, None]
    weights = jax.nn.softmax(scores, axis=-1).astype(jnp.bfloat16)
    blended = jnp.einsum('whqk,wkhd->wqhd', weights.astype(jnp.float32), unpacked[:, :, 2], precision=lax.Precision.HIGHEST)
    return blended.reshape(window_count, window_size, channels).astype(jnp.bfloat16)

def attention_forward(field, w_qkv, w_out, mask_bias, lat_win, lon_win):
    normed, norm_back = jax.vjp(normalize, field)
    blocks = windows(normed, lat_win, lon_win)
    window_count, window_size, channels = blocks.shape
    flat_rows = blocks.reshape(window_count * window_size, channels)
    triple = project(flat_rows, w_qkv).astype(jnp.bfloat16).reshape(window_count, window_size, 3 * channels)
    blended, core_back = jax.vjp(lambda packed: attend(packed, mask_bias), triple)
    blended_flat = blended.reshape(window_count * window_size, channels)
    result = project(blended_flat, w_out).astype(jnp.bfloat16)
    result = unwindows(result.reshape(window_count, window_size, channels), field.shape, lat_win, lon_win)
    return (result, (flat_rows, blended_flat, norm_back, core_back))

def attention_backward(cotan, stored, w_qkv, w_out, grid_shape, lat_win, lon_win):
    flat_rows, blended_flat, norm_back, core_back = stored
    blocks = windows(cotan, lat_win, lon_win)
    window_count, window_size, channels = blocks.shape
    cotan_flat = blocks.reshape(window_count * window_size, channels)
    grad_out = grad_weight(cotan_flat, blended_flat)
    cotan_blended = pull_back(cotan_flat, w_out).reshape(window_count, window_size, channels)
    cotan_triple, = core_back(cotan_blended)
    triple_flat = cotan_triple.reshape(window_count * window_size, 3 * channels)
    grad_qkv = grad_weight(triple_flat, flat_rows)
    cotan_normed = pull_back(triple_flat, w_qkv).reshape(window_count, window_size, channels)
    cotan_field, = norm_back(unwindows(cotan_normed, grid_shape, lat_win, lon_win))
    return (cotan_field, (grad_qkv, grad_out))

def reference(tokens, qkv_first, out_first, qkv_second, out_second, merge_weight, qkv_third, out_third, cotangent):
    grid_shape = tokens.shape
    span = LEV * WA * WO
    no_bias = jnp.zeros((1, span, span), jnp.float32)
    first_out, first_store = attention_forward(tokens, qkv_first, out_first, no_bias, WA, WO)
    layer_one = combine(tokens, first_out)
    rolled = jnp.roll(layer_one, (-(WA // 2), -(WO // 2)), axis=(1, 2))
    mask_bias = region_bias(0, LAT, grid_shape, WA, WO)
    second_out, second_store = attention_forward(rolled, qkv_second, out_second, mask_bias, WA, WO)
    layer_two = combine(layer_one, jnp.roll(second_out, (WA // 2, WO // 2), axis=(1, 2)))
    merged = merge_patches(layer_two)
    normed, norm_back = jax.vjp(normalize, merged)
    merged_shape = normed.shape
    merged_rows = normed.reshape(-1, merged_shape[3])
    hidden = project(merged_rows, merge_weight).astype(jnp.bfloat16)
    hidden = hidden.reshape(merged_shape[0], merged_shape[1], merged_shape[2], -1)
    third_out, third_store = attention_forward(hidden, qkv_third, out_third, no_bias, WA, WO)
    latent = combine(hidden, third_out)
    third_cotan, third_grads = attention_backward(cotangent, third_store, qkv_third, out_third, hidden.shape, WA, WO)
    hidden_cotan = combine(cotangent, third_cotan)
    hidden_rows = hidden_cotan.reshape(-1, hidden.shape[3])
    merge_grad = grad_weight(hidden_rows, merged_rows)
    normed_cotan = pull_back(hidden_rows, merge_weight).reshape(merged_shape)
    merged_cotan, = norm_back(normed_cotan)
    two_cotan = split_patches(merged_cotan)
    second_cotan = jnp.roll(two_cotan, (-(WA // 2), -(WO // 2)), axis=(1, 2))
    rolled_cotan, second_grads = attention_backward(second_cotan, second_store, qkv_second, out_second, grid_shape, WA, WO)
    one_cotan = combine(two_cotan, jnp.roll(rolled_cotan, (WA // 2, WO // 2), axis=(1, 2)))
    first_cotan, first_grads = attention_backward(one_cotan, first_store, qkv_first, out_first, grid_shape, WA, WO)
    tokens_grad = combine(one_cotan, first_cotan)
    return (latent, tokens_grad, first_grads[0], first_grads[1], second_grads[0], second_grads[1], merge_grad, third_grads[0], third_grads[1])
```

```python
import functools

import jax
import jax.numpy as jnp
import numpy as np
from jax import lax
from jax.experimental import pallas as pl
from jax.experimental.pallas import tpu as pltpu
from jax.sharding import Mesh, PartitionSpec as P

F32 = jnp.float32
BF16 = jnp.bfloat16
HDIM = 64
PAIR = 2 * HDIM
SCALE = HDIM ** (-0.5)
WA = 6
WO = 12
ROWS = 12
COLS = 24
TOK = ROWS * COLS
BAND = WA * COLS
C1 = 512
C2 = 1024
M_ROWS = 6
M_COLS = 12
M_TOK = M_ROWS * M_COLS
M_PAD = 80
STRIP_A = 64
STRIP_B = 64
STRIP_D = 32
STRIPS = STRIP_A + STRIP_B + STRIP_D
EPSILON = 1e-05
FAR = -1e30

NN = (((1,), (0,)), ((), ()))
NT = (((1,), (1,)), ((), ()))
TN = (((0,), (0,)), ((), ()))

LAT = ("x", "zh")
LON = ("zl", "y", "c")
DEPTH = ("zh", "zl")
CHIPS = ("x", "zh", "zl", "y")
EVERY = ("x", "zh", "zl", "y", "c")

A_CT = 0
A_O = A_CT + C2
A_DT = A_O + C2
A_N = A_DT + 3 * C2
A_HC = A_N + C2
A_NM = A_HC + C2
A_ALL = A_NM + 2 * C2


def routing():
    pack = np.zeros((STRIPS, TOK), np.float32)
    keep = np.zeros((TOK, TOK), np.float32)
    place = np.zeros((TOK, STRIPS), np.float32)
    half_a, half_o = WA // 2, WO // 2
    count = {"a": 0, "b": STRIP_A, "d": STRIP_A + STRIP_B}
    for r in range(ROWS):
        for c in range(COLS):
            gr, gc = r + half_a, c + half_o
            src = (gr % ROWS) * COLS + gc % COLS
            dst = r * COLS + c
            if gr < ROWS and gc < COLS:
                keep[dst, src] = 1
                continue
            kind = "a" if gc < COLS else ("b" if gr < ROWS else "d")
            slot = count[kind]
            count[kind] += 1
            pack[slot, src] = 1
            place[dst, slot] = 1
    patch = np.zeros((4 * M_PAD, TOK), np.float32)
    for part in range(4):
        for i in range(M_ROWS):
            for j in range(M_COLS):
                src = (2 * i + part % 2) * COLS + 2 * j + part // 2
                patch[part * M_PAD + i * M_COLS + j, src] = 1
    return [m.astype(jnp.bfloat16) for m in (pack, keep, place, patch)]


def dot(a, b, dims):
    return lax.dot_general(a, b, dims, preferred_element_type=F32)


def norm(field):
    values = field.astype(F32)
    centered = values - jnp.mean(values, axis=-1, keepdims=True)
    inverse = lax.rsqrt(jnp.mean(centered * centered, axis=-1, keepdims=True) + EPSILON)
    return centered * inverse, inverse


def norm_back(cotan, unit, inverse):
    cotan = cotan.astype(F32)
    along = jnp.mean(cotan * unit, axis=-1, keepdims=True)
    return (inverse * (cotan - jnp.mean(cotan, axis=-1, keepdims=True) - unit * along)).astype(BF16)


def add(a, b):
    return (a.astype(F32) + b.astype(F32)).astype(BF16)


def stacked(block):
    lane = lax.broadcasted_iota(jnp.int32, (1, PAIR), 1)
    first = jnp.where(lane < HDIM, 1.0, 0.0).astype(BF16)
    second = jnp.where(lane < HDIM, 0.0, 1.0).astype(BF16)
    return jnp.concatenate([block * first, block * second], axis=0)


def joined(both):
    size = both.shape[0] // 2
    lane = lax.broadcasted_iota(jnp.int32, (size, PAIR), 1)
    return jnp.where(lane < HDIM, both[:size], both[size:])


def softmax(queries, keys, bias):
    scores = dot(queries, keys, NT) * SCALE + bias
    raised = jnp.exp(scores - jnp.max(scores, axis=-1, keepdims=True))
    return raised * (1.0 / jnp.sum(raised, axis=-1, keepdims=True))


def attend(qkv_ref, o_ref, channels, spans, biases):
    for (start, size), bias in zip(spans, biases):
        rows = pl.ds(start, size)
        for pair in range(channels // PAIR):
            lanes = pair * PAIR
            q = stacked(qkv_ref[rows, lanes : lanes + PAIR])
            k = qkv_ref[rows, channels + lanes : channels + lanes + PAIR]
            v = qkv_ref[rows, 2 * channels + lanes : 2 * channels + lanes + PAIR]
            p = softmax(q, k, bias).astype(BF16)
            o_ref[rows, lanes : lanes + PAIR] = joined(dot(p, v, NN)).astype(BF16)


def attend_back(qkv_ref, do_ref, dqkv_ref, channels, spans, biases):
    for (start, size), bias in zip(spans, biases):
        rows = pl.ds(start, size)
        for pair in range(channels // PAIR):
            lanes = pair * PAIR
            q = stacked(qkv_ref[rows, lanes : lanes + PAIR])
            k = qkv_ref[rows, channels + lanes : channels + lanes + PAIR]
            v = qkv_ref[rows, 2 * channels + lanes : 2 * channels + lanes + PAIR]
            do = stacked(do_ref[rows, lanes : lanes + PAIR])
            p = softmax(q, k, bias)
            dp = dot(do, v, NT)
            inner = jnp.sum(p * dp, axis=-1, keepdims=True)
            ds = (p * (dp - inner) * SCALE).astype(BF16)
            dq = joined(dot(ds, k, NN))
            dk = dot(ds, q, TN)
            dv = dot(p.astype(BF16), do, TN)
            dqkv_ref[rows, lanes : lanes + PAIR] = dq.astype(BF16)
            dqkv_ref[rows, channels + lanes : channels + lanes + PAIR] = dk.astype(BF16)
            dqkv_ref[rows, 2 * channels + lanes : 2 * channels + lanes + PAIR] = dv.astype(BF16)


BANDS = [(0, BAND), (BAND, BAND)]


def band_biases(last_lat):
    def ids(dim, shape):
        token = lax.broadcasted_iota(jnp.int32, shape, dim)
        row = (token * 171) >> 12
        col = token - COLS * row
        return jnp.where(col >= WO, 1.0, 0.0), jnp.where(row >= WA // 2, 2.0, 0.0)

    win_q, half_q = ids(0, (BAND, BAND))
    win_k, half_k = ids(1, (BAND, BAND))
    plain = jnp.where(win_q == win_k, 0.0, FAR)
    plain = jnp.concatenate([plain, plain], axis=0)
    if last_lat is None:
        return [plain, plain]
    cut = jnp.where(win_q + half_q == win_k + half_k, 0.0, FAR)
    cut = jnp.concatenate([cut, cut], axis=0)
    return [plain, jnp.where(last_lat == 1, cut, plain)]


def first_forward(tok_ref, wqkv_ref, wo_ref, pack_ref, one_ref, strips_ref, qkv_ref, o_ref):
    unit, _ = norm(tok_ref[...])
    qkv_ref[...] = dot(unit.astype(BF16), wqkv_ref[...], NT).astype(BF16)
    attend(qkv_ref, o_ref, C1, BANDS, band_biases(None))
    out = dot(o_ref[...], wo_ref[...], NT).astype(BF16)
    one = add(tok_ref[...], out)
    one_ref[...] = one
    strips_ref[...] = dot(pack_ref[...], one, NN).astype(BF16)


def second_forward(
    last_ref, one_ref, in_a, in_b, in_d, wqkv_ref, wo_ref, keep_ref, place_ref,
    rolled_ref, own_ref, strips_ref, qkv_ref, o_ref,
):
    arrived = jnp.concatenate([in_a[...], in_b[...], in_d[...]], axis=0)
    rolled = (dot(keep_ref[...], one_ref[...], NN) + dot(place_ref[...], arrived, NN)).astype(BF16)
    rolled_ref[...] = rolled
    unit, _ = norm(rolled)
    qkv_ref[...] = dot(unit.astype(BF16), wqkv_ref[...], NT).astype(BF16)
    attend(qkv_ref, o_ref, C1, BANDS, band_biases(last_ref[0]))
    out = dot(o_ref[...], wo_ref[...], NT).astype(BF16)
    own_ref[...] = dot(keep_ref[...], out, TN).astype(BF16)
    strips_ref[...] = dot(place_ref[...], out, TN).astype(BF16)


def third_both(
    one_ref, own_ref, in_a, in_b, in_d, ct_ref, wm_ref, wqkv_ref, wo_ref, pack_ref, patch_ref,
    latent_ref, two_cot_ref, strips_ref, acts_ref,
    wide, qkv_ref, do_ref,
):
    arrived = jnp.concatenate([in_a[...], in_b[...], in_d[...]], axis=0)
    out_two = own_ref[...].astype(F32) + dot(pack_ref[...], arrived, TN)
    two = (one_ref[...].astype(F32) + out_two).astype(BF16)
    parts = dot(patch_ref[...], two, NN)
    merged = jnp.concatenate([parts[p * M_PAD : (p + 1) * M_PAD] for p in range(4)], axis=1)
    unit_m, inverse_m = norm(merged)
    acts_ref[:, A_NM : A_NM + 2 * C2] = unit_m.astype(BF16)
    hidden = dot(acts_ref[:, A_NM : A_NM + 2 * C2], wm_ref[...], NT).astype(BF16)
    unit_h, inverse_h = norm(hidden)
    acts_ref[:, A_N : A_N + C2] = unit_h.astype(BF16)
    qkv_ref[...] = dot(acts_ref[:, A_N : A_N + C2], wqkv_ref[...], NT).astype(BF16)
    key = lax.broadcasted_iota(jnp.int32, (2 * M_PAD, M_PAD), 1)
    bias = jnp.where(key < M_TOK, 0.0, FAR)
    span = [(0, M_PAD)]
    attend(qkv_ref, acts_ref.at[:, A_O : A_O + C2], C2, span, [bias])
    out = dot(acts_ref[:, A_O : A_O + C2], wo_ref[...], NT).astype(BF16)
    wide[...] = hidden.astype(F32) + out.astype(F32)
    for i in range(M_ROWS):
        latent_ref[i] = wide[i * M_COLS : (i + 1) * M_COLS, :].astype(BF16)
    wide[M_TOK:, :] = jnp.zeros((M_PAD - M_TOK, C2), F32)
    for i in range(M_ROWS):
        wide[i * M_COLS : (i + 1) * M_COLS, :] = ct_ref[i].astype(F32)
    cot = wide[...].astype(BF16)
    acts_ref[:, A_CT : A_CT + C2] = cot
    do_ref[...] = dot(cot, wo_ref[...], NN).astype(BF16)
    attend_back(qkv_ref, do_ref, acts_ref.at[:, A_DT : A_DT + 3 * C2], C2, span, [bias])
    dn = dot(acts_ref[:, A_DT : A_DT + 3 * C2], wqkv_ref[...], NN).astype(BF16)
    hidden_cot = add(cot, norm_back(dn, unit_h, inverse_h))
    acts_ref[:, A_HC : A_HC + C2] = hidden_cot
    dnm = dot(hidden_cot, wm_ref[...], NN).astype(BF16)
    merged_cot = norm_back(dnm, unit_m, inverse_m)
    two_cot = dot(patch_ref[0:M_PAD, :], merged_cot[:, 0:C1], TN)
    for p in range(1, 4):
        two_cot = two_cot + dot(
            patch_ref[p * M_PAD : (p + 1) * M_PAD, :], merged_cot[:, p * C1 : (p + 1) * C1], TN
        )
    two_cot = two_cot.astype(BF16)
    two_cot_ref[...] = two_cot
    strips_ref[...] = dot(pack_ref[...], two_cot, NN).astype(BF16)


T_ROWS = 96


def third_grads(core_ref, mine_ref, other_ref, out_ref):
    core = core_ref[0]
    half = C2 // 2

    def both(start, width):
        where = pl.ds(start, width)
        return jnp.concatenate([mine_ref[:, where], other_ref[:, where]], axis=0)

    n = both(pl.multiple_of(A_N + core * half, half), half)
    o = both(pl.multiple_of(A_O + core * half, half), half)
    nm = both(pl.multiple_of(A_NM + core * C2, C2), C2)
    for piece in range(8):
        step = 3 * C2 // 8
        grad = dot(both(A_DT + piece * step, step), n, TN).astype(BF16)
        out_ref[piece * 8 : piece * 8 + 8, 0:48] = grad.reshape(8, 48, half)
    for piece in range(4):
        step = C2 // 4
        chips = slice(piece * 16, piece * 16 + 16)
        grad = dot(both(A_CT + piece * step, step), o, TN).astype(BF16)
        out_ref[chips, 48:64] = grad.reshape(16, 16, half)
        hc = both(A_HC + piece * step, step)
        for side in range(2):
            grad = dot(hc, nm[:, side * half : side * half + half], TN).astype(BF16)
            out_ref[chips, 64 + 16 * side : 80 + 16 * side] = grad.reshape(16, 16, half)


S_ROWS = 32


def block_grads(core, dqkv_ref, unit_ref, cot, o_ref, keep_out, send_out):
    half = C1 // 2
    for ref, side in ((keep_out, core), (send_out, 1 - core)):
        where = pl.ds(pl.multiple_of(side * half, half), half)
        grad_qkv = dot(dqkv_ref[...], unit_ref[:, where], TN).reshape(64, 24, half)
        grad_out = dot(cot, o_ref[:, where], TN).reshape(64, 8, half)
        ref[...] = jnp.concatenate([grad_qkv, grad_out], axis=1).astype(BF16)


def second_back(
    last_ref, core_ref, two_cot_ref, in_a, in_b, in_d, rolled_ref, qkv_ref, o_ref, wqkv_ref, wo_ref,
    keep_ref, place_ref,
    own_ref, strips_ref, grad_keep, grad_send,
    do_ref, dqkv_ref, unit_ref,
):
    arrived = jnp.concatenate([in_a[...], in_b[...], in_d[...]], axis=0)
    cot = (dot(keep_ref[...], two_cot_ref[...], NN) + dot(place_ref[...], arrived, NN)).astype(BF16)
    unit, inverse = norm(rolled_ref[...])
    unit_ref[...] = unit.astype(BF16)
    do_ref[...] = dot(cot, wo_ref[...], NN).astype(BF16)
    attend_back(qkv_ref, do_ref, dqkv_ref, C1, BANDS, band_biases(last_ref[0]))
    dn = dot(dqkv_ref[...], wqkv_ref[...], NN).astype(BF16)
    rolled_cot = norm_back(dn, unit, inverse)
    own_ref[...] = dot(keep_ref[...], rolled_cot, TN).astype(BF16)
    strips_ref[...] = dot(place_ref[...], rolled_cot, TN).astype(BF16)
    block_grads(core_ref[0], dqkv_ref, unit_ref, cot, o_ref, grad_keep, grad_send)


def first_back(
    core_ref, two_cot_ref, own_ref, in_a, in_b, in_d, tok_ref, qkv_ref, o_ref, wqkv_ref, wo_ref, pack_ref,
    grad_ref, grad_keep, grad_send,
    do_ref, dqkv_ref, unit_ref,
):
    arrived = jnp.concatenate([in_a[...], in_b[...], in_d[...]], axis=0)
    back = own_ref[...].astype(F32) + dot(pack_ref[...], arrived, TN)
    cot = (two_cot_ref[...].astype(F32) + back).astype(BF16)
    unit, inverse = norm(tok_ref[...])
    unit_ref[...] = unit.astype(BF16)
    do_ref[...] = dot(cot, wo_ref[...], NN).astype(BF16)
    attend_back(qkv_ref, do_ref, dqkv_ref, C1, BANDS, band_biases(None))
    dn = dot(dqkv_ref[...], wqkv_ref[...], NN).astype(BF16)
    grad_ref[...] = add(cot, norm_back(dn, unit, inverse))
    block_grads(core_ref[0], dqkv_ref, unit_ref, cot, o_ref, grad_keep, grad_send)


VMEM = pl.BlockSpec(memory_space=pltpu.VMEM)
SMEM = pl.BlockSpec(memory_space=pltpu.SMEM)


def call(kernel, name, scalars, arrays, outs, scratch=(), flops=10**9, limit=56):
    moved = sum(a.size * a.dtype.itemsize for a in arrays)
    moved += sum(int(np.prod(s)) * 2 for s in outs)
    return pl.pallas_call(
        kernel,
        name=name,
        out_shape=[jax.ShapeDtypeStruct(s, BF16) for s in outs],
        in_specs=[SMEM] * len(scalars) + [VMEM] * len(arrays),
        out_specs=[VMEM] * len(outs),
        scratch_shapes=[pltpu.VMEM(s, d) for s, d in scratch],
        cost_estimate=pl.CostEstimate(flops=flops, bytes_accessed=moved, transcendentals=0),
        compiler_params=pltpu.CompilerParams(vmem_limit_bytes=limit * 2**20),
    )(*scalars, *arrays)


def send_strips(strips, step):
    lats, lons = 8, 16

    def route(lat_step, lon_step):
        return [
            (a * lons + o, (a + lat_step) % lats * lons + (o + lon_step) % lons)
            for a in range(lats)
            for o in range(lons)
        ]

    a = lax.ppermute(strips[:STRIP_A], EVERY, route(step, 0))
    b = lax.ppermute(strips[STRIP_A : STRIP_A + STRIP_B], EVERY, route(0, step))
    d = lax.ppermute(strips[STRIP_A + STRIP_B :], EVERY, route(step, step))
    return a, b, d


def other_core(block):
    return lax.ppermute(block, "c", [(0, 1), (1, 0)])


def over_chips(block):
    block = lax.psum_scatter(block, "x", scatter_dimension=0, tiled=True)
    block = lax.psum_scatter(block, DEPTH, scatter_dimension=0, tiled=True)
    return lax.psum_scatter(block, "y", scatter_dimension=0, tiled=True)[0]


def exchange_chips(block):
    block = lax.all_to_all(block, CHIPS, split_axis=0, concat_axis=0, tiled=True)
    return jnp.sum(block.astype(F32), axis=0)


def on_device(
    tokens, qkv_first, out_first, qkv_second, out_second, merge_weight, qkv_third, out_third, cotangent
):
    pack, keep, place, patch = (jnp.asarray(m) for m in routing())
    core = lax.axis_index("c").astype(jnp.int32)
    core_s = core.reshape(1)
    last = (lax.axis_index(LAT) == 7).astype(jnp.int32).reshape(1)
    tok = tokens.reshape(TOK, C1)
    wide, slim = (TOK, 3 * C1), (TOK, C1)
    one, strips, qkv1, o1 = call(
        first_forward, "first_forward", [], [tok, qkv_first, out_first, pack],
        [slim, (STRIPS, C1), wide, slim],
    )
    arrived = send_strips(strips, -1)
    rolled, own, strips, qkv2, o2 = call(
        second_forward, "second_forward", [last], [one, *arrived, qkv_second, out_second, keep, place],
        [slim, slim, (STRIPS, C1), wide, slim],
    )
    arrived = send_strips(strips, 1)
    latent, two_cot, strips, acts = call(
        third_both, "third_both", [],
        [one, own, *arrived, cotangent[0], merge_weight, qkv_third, out_third, pack, patch],
        [(M_ROWS, M_COLS, C2), slim, (STRIPS, C1), (M_PAD, A_ALL)],
        [((M_PAD, C2), F32), ((M_PAD, 3 * C2), BF16), ((M_PAD, C2), BF16)],
    )
    arrived = send_strips(strips, -1)
    acts_other = other_core(acts)
    (grads_t,) = call(third_grads, "third_grads", [core_s], [acts, acts_other], [(64, T_ROWS, C2 // 2)])
    share_t = over_chips(grads_t)
    back_scratch = [(slim, BF16), (wide, BF16), (slim, BF16)]
    half = (64, S_ROWS, C1 // 2)
    own, strips, keep2, send2 = call(
        second_back, "second_back", [last, core_s],
        [two_cot, *arrived, rolled, qkv2, o2, qkv_second, out_second, keep, place],
        [slim, (STRIPS, C1), half, half], back_scratch,
    )
    arrived = send_strips(strips, 1)
    tokens_grad, keep1, send1 = call(
        first_back, "first_back", [core_s],
        [two_cot, own, *arrived, tok, qkv1, o1, qkv_first, out_first, pack],
        [slim, half, half], back_scratch,
    )
    share_s = exchange_chips(add(keep2, other_core(send2)))
    share_f = exchange_chips(add(keep1, other_core(send1)))

    share_t = share_t.astype(F32)

    def halves(share, rows, start):
        block = share[start : start + 2 * rows].reshape(2, rows, -1)
        return block

    t_q = halves(share_t, 24, 0)
    t_o = halves(share_t, 8, 48)
    t_m = jnp.concatenate([halves(share_t, 8, 64), halves(share_t, 8, 80)], axis=2)
    s_q, s_o = halves(share_s, 12, 0), halves(share_s, 4, 24)
    f_q, f_o = halves(share_f, 12, 0), halves(share_f, 4, 24)
    shares = [f_q, f_o, s_q, s_o, t_m, t_q, t_o]
    flat = jnp.concatenate([s.reshape(2, -1, 256) for s in shares], axis=1).astype(BF16)
    mine = lax.dynamic_index_in_dim(flat, core, 0, keepdims=False)
    given = other_core(lax.dynamic_index_in_dim(flat, 1 - core, 0, keepdims=False))
    outs, at = [], 0
    for s in shares:
        rows, width = s.shape[1:]
        count = rows * width // 256
        low = mine[at : at + count].reshape(rows, width)
        high = given[at : at + count].reshape(rows, width)
        at += count
        outs.append(
            jnp.where(
                core == 0,
                jnp.concatenate([low, high], axis=1),
                jnp.concatenate([high, low], axis=1),
            ).astype(F32)
        )
    return (latent[None], tokens_grad.reshape(tokens.shape), *outs)


def solution(mesh):
    split = Mesh(mesh.devices.reshape(4, 2, 2, 4, 2), EVERY)
    grid = P(None, LAT, LON, None)
    return jax.shard_map(
        on_device,
        mesh=split,
        in_specs=(grid,) + (P(),) * 7 + (grid,),
        out_specs=(grid, grid) + (P(EVERY, None),) * 7,
        check_vma=False,
    )
```

```python
import jax
import jax.numpy as jnp
import numpy as np
from jax import lax
from jax.experimental import pallas as pl
from jax.experimental.pallas import tpu as pltpu
from jax.sharding import Mesh, PartitionSpec as P

F32 = jnp.float32
BF16 = jnp.bfloat16
HDIM = 64
PAIR = 2 * HDIM
SCALE = HDIM ** (-0.5)
WA = 6
WO = 12
ROWS = 12
COLS = 24
TOK = ROWS * COLS
BAND = WA * COLS
C1 = 512
C2 = 1024
M_ROWS = 6
M_COLS = 12
M_TOK = M_ROWS * M_COLS
M_PAD = 80
STRIP_A = 64
STRIP_B = 64
STRIP_D = 32
STRIPS = STRIP_A + STRIP_B + STRIP_D
EPSILON = 1e-05
FAR = -1e30

NN = (((1,), (0,)), ((), ()))
NT = (((1,), (1,)), ((), ()))
TN = (((0,), (0,)), ((), ()))

LAT = ("x", "zh")
LON = ("zl", "y", "c")
DEPTH = ("zh", "zl")
CHIPS = ("x", "zh", "zl", "y")
EVERY = ("x", "zh", "zl", "y", "c")

A_CT = 0
A_O = A_CT + C2
A_DT = A_O + C2
A_N = A_DT + 3 * C2
A_HC = A_N + C2
A_NM = A_HC + C2
A_ALL = A_NM + 2 * C2


def routing():
    pack = np.zeros((STRIPS, TOK), np.float32)
    keep = np.zeros((TOK, TOK), np.float32)
    place = np.zeros((TOK, STRIPS), np.float32)
    half_a, half_o = WA // 2, WO // 2
    count = {"a": 0, "b": STRIP_A, "d": STRIP_A + STRIP_B}
    for r in range(ROWS):
        for c in range(COLS):
            gr, gc = r + half_a, c + half_o
            src = (gr % ROWS) * COLS + gc % COLS
            dst = r * COLS + c
            if gr < ROWS and gc < COLS:
                keep[dst, src] = 1
                continue
            kind = "a" if gc < COLS else ("b" if gr < ROWS else "d")
            slot = count[kind]
            count[kind] += 1
            pack[slot, src] = 1
            place[dst, slot] = 1
    patch = np.zeros((4 * M_PAD, TOK), np.float32)
    for part in range(4):
        for i in range(M_ROWS):
            for j in range(M_COLS):
                src = (2 * i + part % 2) * COLS + 2 * j + part // 2
                patch[part * M_PAD + i * M_COLS + j, src] = 1
    return [m.astype(jnp.bfloat16) for m in (pack, keep, place, patch)]


def dot(a, b, dims):
    return lax.dot_general(a, b, dims, preferred_element_type=F32)


def norm(field):
    values = field.astype(F32)
    centered = values - jnp.mean(values, axis=-1, keepdims=True)
    inverse = lax.rsqrt(jnp.mean(centered * centered, axis=-1, keepdims=True) + EPSILON)
    return centered * inverse, inverse


def norm_back(cotan, unit, inverse):
    cotan = cotan.astype(F32)
    along = jnp.mean(cotan * unit, axis=-1, keepdims=True)
    return (inverse * (cotan - jnp.mean(cotan, axis=-1, keepdims=True) - unit * along)).astype(BF16)


def add(a, b):
    return (a.astype(F32) + b.astype(F32)).astype(BF16)


def stacked(block):
    lane = lax.broadcasted_iota(jnp.int32, (1, PAIR), 1)
    first = jnp.where(lane < HDIM, 1.0, 0.0).astype(BF16)
    second = jnp.where(lane < HDIM, 0.0, 1.0).astype(BF16)
    return jnp.concatenate([block * first, block * second], axis=0)


def joined(both):
    size = both.shape[0] // 2
    lane = lax.broadcasted_iota(jnp.int32, (size, PAIR), 1)
    return jnp.where(lane < HDIM, both[:size], both[size:])


def softmax(queries, keys, bias):
    scores = dot(queries, keys, NT) * SCALE + bias
    raised = jnp.exp(scores - jnp.max(scores, axis=-1, keepdims=True))
    return raised * (1.0 / jnp.sum(raised, axis=-1, keepdims=True))


def attend(qkv_ref, o_ref, p_ref, channels, spans, biases):
    for n, ((start, size), bias) in enumerate(zip(spans, biases)):
        rows = pl.ds(start, size)
        for pair in range(channels // PAIR):
            lanes = pair * PAIR
            q = stacked(qkv_ref[rows, lanes : lanes + PAIR])
            k = qkv_ref[rows, channels + lanes : channels + lanes + PAIR]
            v = qkv_ref[rows, 2 * channels + lanes : 2 * channels + lanes + PAIR]
            p = softmax(q, k, bias).astype(BF16)
            p_ref[n, pair] = p
            o_ref[rows, lanes : lanes + PAIR] = joined(dot(p, v, NN)).astype(BF16)


def attend_back(qkv_ref, p_ref, do_ref, dqkv_ref, channels, spans):
    for n, (start, size) in enumerate(spans):
        rows = pl.ds(start, size)
        for pair in range(channels // PAIR):
            lanes = pair * PAIR
            q = stacked(qkv_ref[rows, lanes : lanes + PAIR])
            k = qkv_ref[rows, channels + lanes : channels + lanes + PAIR]
            v = qkv_ref[rows, 2 * channels + lanes : 2 * channels + lanes + PAIR]
            do = stacked(do_ref[rows, lanes : lanes + PAIR])
            p = p_ref[n, pair].astype(F32)
            dp = dot(do, v, NT)
            inner = jnp.sum(p * dp, axis=-1, keepdims=True)
            ds = (p * (dp - inner) * SCALE).astype(BF16)
            dq = joined(dot(ds, k, NN))
            dk = dot(ds, q, TN)
            dv = dot(p_ref[n, pair], do, TN)
            dqkv_ref[rows, lanes : lanes + PAIR] = dq.astype(BF16)
            dqkv_ref[rows, channels + lanes : channels + lanes + PAIR] = dk.astype(BF16)
            dqkv_ref[rows, 2 * channels + lanes : 2 * channels + lanes + PAIR] = dv.astype(BF16)


BANDS = [(0, BAND), (BAND, BAND)]


def band_biases(last_lat):
    def ids(dim, shape):
        token = lax.broadcasted_iota(jnp.int32, shape, dim)
        row = (token * 171) >> 12
        col = token - COLS * row
        return jnp.where(col >= WO, 1.0, 0.0), jnp.where(row >= WA // 2, 2.0, 0.0)

    win_q, half_q = ids(0, (BAND, BAND))
    win_k, half_k = ids(1, (BAND, BAND))
    plain = jnp.where(win_q == win_k, 0.0, FAR)
    plain = jnp.concatenate([plain, plain], axis=0)
    if last_lat is None:
        return [plain, plain]
    cut = jnp.where(win_q + half_q == win_k + half_k, 0.0, FAR)
    cut = jnp.concatenate([cut, cut], axis=0)
    return [plain, jnp.where(last_lat == 1, cut, plain)]


def put_strips(refs, strips):
    bounds = (0, STRIP_A, STRIP_A + STRIP_B, STRIPS)
    for ref, low, high in zip(refs, bounds[:-1], bounds[1:]):
        ref[...] = strips[low:high].astype(BF16)
        send(ref)


def send(*refs):
    for ref in refs:
        if isinstance(ref, Stored):
            ref.send()


def get_strips(refs):
    return jnp.concatenate([ref[...] for ref in refs], axis=0)


def first_forward(tok_ref, wqkv_ref, wo_ref, pack_ref, one_ref, out_a, out_b, out_d, qkv_ref, o_ref, p_ref):
    unit, _ = norm(tok_ref[...])
    qkv_ref[...] = dot(unit.astype(BF16), wqkv_ref[...], NT).astype(BF16)
    send(qkv_ref)
    attend(qkv_ref, o_ref, p_ref, C1, BANDS, band_biases(None))
    send(p_ref, o_ref)
    out = dot(o_ref[...], wo_ref[...], NT).astype(BF16)
    one = add(tok_ref[...], out)
    one_ref[...] = one
    put_strips((out_a, out_b, out_d), dot(pack_ref[...], one, NN))


def second_forward(
    last_ref, one_ref, in_a, in_b, in_d, wqkv_ref, wo_ref, keep_ref, place_ref,
    rolled_ref, own_ref, out_a, out_b, out_d, qkv_ref, o_ref, p_ref,
):
    arrived = get_strips((in_a, in_b, in_d))
    rolled = (dot(keep_ref[...], one_ref[...], NN) + dot(place_ref[...], arrived, NN)).astype(BF16)
    rolled_ref[...] = rolled
    unit, _ = norm(rolled)
    qkv_ref[...] = dot(unit.astype(BF16), wqkv_ref[...], NT).astype(BF16)
    send(qkv_ref, rolled_ref)
    attend(qkv_ref, o_ref, p_ref, C1, BANDS, band_biases(last_ref[0]))
    send(p_ref, o_ref)
    out = dot(o_ref[...], wo_ref[...], NT).astype(BF16)
    put_strips((out_a, out_b, out_d), dot(place_ref[...], out, TN))
    own_ref[...] = dot(keep_ref[...], out, TN).astype(BF16)


def third_both(
    one_ref, own_ref, in_a, in_b, in_d, ct_ref, wm_ref, wqkv_ref, wo_ref, pack_ref, patch_ref,
    latent_ref, two_cot_ref, out_a, out_b, out_d, acts_ref,
    wide, qkv_ref, do_ref, p_ref,
):
    arrived = get_strips((in_a, in_b, in_d))
    out_two = own_ref[...].astype(F32) + dot(pack_ref[...], arrived, TN)
    two = (one_ref[...].astype(F32) + out_two).astype(BF16)
    parts = dot(patch_ref[...], two, NN)
    merged = jnp.concatenate([parts[p * M_PAD : (p + 1) * M_PAD] for p in range(4)], axis=1)
    unit_m, inverse_m = norm(merged)
    acts_ref[:, A_NM : A_NM + 2 * C2] = unit_m.astype(BF16)
    hidden = dot(acts_ref[:, A_NM : A_NM + 2 * C2], wm_ref[...], NT).astype(BF16)
    unit_h, inverse_h = norm(hidden)
    acts_ref[:, A_N : A_N + C2] = unit_h.astype(BF16)
    qkv_ref[...] = dot(acts_ref[:, A_N : A_N + C2], wqkv_ref[...], NT).astype(BF16)
    key = lax.broadcasted_iota(jnp.int32, (2 * M_PAD, M_PAD), 1)
    bias = jnp.where(key < M_TOK, 0.0, FAR)
    span = [(0, M_PAD)]
    attend(qkv_ref, acts_ref.at[:, A_O : A_O + C2], p_ref, C2, span, [bias])
    out = dot(acts_ref[:, A_O : A_O + C2], wo_ref[...], NT).astype(BF16)
    wide[...] = hidden.astype(F32) + out.astype(F32)
    for i in range(M_ROWS):
        latent_ref[i] = wide[i * M_COLS : (i + 1) * M_COLS, :].astype(BF16)
    send(latent_ref)
    wide[M_TOK:, :] = jnp.zeros((M_PAD - M_TOK, C2), F32)
    for i in range(M_ROWS):
        wide[i * M_COLS : (i + 1) * M_COLS, :] = ct_ref[i].astype(F32)
    cot = wide[...].astype(BF16)
    acts_ref[:, A_CT : A_CT + C2] = cot
    do_ref[...] = dot(cot, wo_ref[...], NN).astype(BF16)
    attend_back(qkv_ref, p_ref, do_ref, acts_ref.at[:, A_DT : A_DT + 3 * C2], C2, span)
    dn = dot(acts_ref[:, A_DT : A_DT + 3 * C2], wqkv_ref[...], NN).astype(BF16)
    hidden_cot = add(cot, norm_back(dn, unit_h, inverse_h))
    acts_ref[:, A_HC : A_HC + C2] = hidden_cot
    send(acts_ref)
    dnm = dot(hidden_cot, wm_ref[...], NN).astype(BF16)
    merged_cot = norm_back(dnm, unit_m, inverse_m)
    two_cot = dot(patch_ref[0:M_PAD, :], merged_cot[:, 0:C1], TN)
    for p in range(1, 4):
        two_cot = two_cot + dot(
            patch_ref[p * M_PAD : (p + 1) * M_PAD, :], merged_cot[:, p * C1 : (p + 1) * C1], TN
        )
    two_cot = two_cot.astype(BF16)
    two_cot_ref[...] = two_cot
    send(two_cot_ref)
    put_strips((out_a, out_b, out_d), dot(pack_ref[...], two_cot, NN))


def both_cores(mine_ref, other_ref, start, width):
    where = pl.ds(start, width)
    return jnp.concatenate([mine_ref[:, where], other_ref[:, where]], axis=0)


def attention_grads(core_ref, mine_ref, other_ref, out_ref):
    half = C2 // 2
    n = both_cores(mine_ref, other_ref, pl.multiple_of(A_N + core_ref[0] * half, half), half)
    o = both_cores(mine_ref, other_ref, pl.multiple_of(A_O + core_ref[0] * half, half), half)
    for piece in range(8):
        step = 3 * C2 // 8
        grad = dot(both_cores(mine_ref, other_ref, A_DT + piece * step, step), n, TN).astype(BF16)
        out_ref[piece * 8 : piece * 8 + 8, 0:48] = grad.reshape(8, 48, half)
    for piece in range(4):
        step = C2 // 4
        grad = dot(both_cores(mine_ref, other_ref, A_CT + piece * step, step), o, TN).astype(BF16)
        out_ref[piece * 16 : piece * 16 + 16, 48:64] = grad.reshape(16, 16, half)


def merge_grads(core_ref, y_ref, mine_ref, other_ref, out_0, out_1, out_2, out_3, all_ref):
    half = C2 // 2
    nm = both_cores(mine_ref, other_ref, pl.multiple_of(A_NM + core_ref[0] * C2, C2), C2)
    for piece in range(4):
        step = C2 // 4
        hc = both_cores(mine_ref, other_ref, A_HC + piece * step, step)
        for side in range(2):
            grad = dot(hc, nm[:, side * half : side * half + half], TN).astype(BF16).reshape(4, 4, 16, half)
            for y in range(4):
                all_ref[y, piece * 4 : piece * 4 + 4, 16 * side : 16 * side + 16] = grad[:, y]
    for d, ref in enumerate((out_0, out_1, out_2, out_3)):
        ref[...] = all_ref[(y_ref[0] + d) % 4]


def sum_of(refs):
    total = refs[0][...].astype(F32)
    for ref in refs[1:]:
        total = total + ref[...].astype(F32)
    return total


def second_pieces(z_ref, x_ref, q_ref, m_0, m_1, m_2, m_3, q_out0, q_out1, q_out2, q_out3, o_0, o_1, o_2, o_3, m_ref):
    m_ref[...] = sum_of((m_0, m_1, m_2, m_3)).astype(BF16).reshape(4, 4, 32, C2 // 2)
    for d, (q, m) in enumerate(zip((q_out0, q_out1, q_out2, q_out3), (o_0, o_1, o_2, o_3))):
        q[...] = q_ref[(z_ref[0] + d) % 4]
        m[...] = m_ref[(x_ref[0] + d) % 4]


def last_pieces(
    y_ref, z_ref, q_0, q_1, q_2, q_3, m_0, m_1, m_2, m_3, p_0, p_1, p_2, p_3, o_0, o_1, o_2, o_3, q_ref, m_ref
):
    q_ref[...] = sum_of((q_0, q_1, q_2, q_3)).astype(BF16)
    m_ref[...] = sum_of((m_0, m_1, m_2, m_3)).astype(BF16)
    for d, (q, m) in enumerate(zip((p_0, p_1, p_2, p_3), (o_0, o_1, o_2, o_3))):
        q[...] = q_ref[(y_ref[0] + d) % 4]
        m[...] = m_ref[(z_ref[0] + d) % 4]


def pack_pairs(mine_s, other_s, mine_f, other_f, out_ref):
    out_ref[:, 0:32] = add(mine_s[...], other_s[...])
    out_ref[:, 32:64] = add(mine_f[...], other_f[...])


def block_grads(core_ref, dqkv_ref, unit_ref, cot_ref, o_ref, keep_out, send_out):
    half = C1 // 2
    for ref, side in ((send_out, 1 - core_ref[0]), (keep_out, core_ref[0])):
        where = pl.ds(pl.multiple_of(side * half, half), half)
        grad_qkv = dot(dqkv_ref[...], unit_ref[:, where], TN).reshape(64, 24, half)
        grad_out = dot(cot_ref[...], o_ref[:, where], TN).reshape(64, 8, half)
        ref[...] = jnp.concatenate([grad_qkv, grad_out], axis=1).astype(BF16)
        send(ref)


def second_back(
    two_cot_ref, in_a, in_b, in_d, rolled_ref, qkv_ref, p_ref, wqkv_ref, wo_ref, keep_ref, place_ref,
    own_ref, out_a, out_b, out_d, dqkv_ref, unit_ref, cot_ref,
    do_ref,
):
    arrived = get_strips((in_a, in_b, in_d))
    cot = (dot(keep_ref[...], two_cot_ref[...], NN) + dot(place_ref[...], arrived, NN)).astype(BF16)
    cot_ref[...] = cot
    unit, inverse = norm(rolled_ref[...])
    unit_ref[...] = unit.astype(BF16)
    do_ref[...] = dot(cot, wo_ref[...], NN).astype(BF16)
    attend_back(qkv_ref, p_ref, do_ref, dqkv_ref, C1, BANDS)
    send(unit_ref, cot_ref, dqkv_ref)
    dn = dot(dqkv_ref[...], wqkv_ref[...], NN).astype(BF16)
    rolled_cot = norm_back(dn, unit, inverse)
    put_strips((out_a, out_b, out_d), dot(place_ref[...], rolled_cot, TN))
    own_ref[...] = dot(keep_ref[...], rolled_cot, TN).astype(BF16)


def first_back(
    core_ref, two_cot_ref, own_ref, in_a, in_b, in_d, tok_ref, qkv_ref, p_ref, o_ref, wo_ref, pack_ref,
    cot_ref, dqkv_ref, grad_keep, grad_send,
    do_ref, unit_ref,
):
    arrived = get_strips((in_a, in_b, in_d))
    back = own_ref[...].astype(F32) + dot(pack_ref[...], arrived, TN)
    cot = (two_cot_ref[...].astype(F32) + back).astype(BF16)
    cot_ref[...] = cot
    unit_ref[...] = norm(tok_ref[...])[0].astype(BF16)
    do_ref[...] = dot(cot, wo_ref[...], NN).astype(BF16)
    attend_back(qkv_ref, p_ref, do_ref, dqkv_ref, C1, BANDS)
    send(cot_ref, dqkv_ref)
    block_grads(core_ref, dqkv_ref, unit_ref, cot_ref, o_ref, grad_keep, grad_send)


def first_input(cot_ref, dqkv_ref, tok_ref, wqkv_ref, grad_ref):
    unit, inverse = norm(tok_ref[...])
    dn = dot(dqkv_ref[...], wqkv_ref[...], NN).astype(BF16)
    grad_ref[...] = add(cot_ref[...], norm_back(dn, unit, inverse))


def split_cores(core, total, rows, at, keep_ref, send_ref, here):
    low, high = total[at : at + rows], total[at + rows : at + 2 * rows]
    keep_ref[here : here + rows] = jnp.where(core == 0, low, high)
    send_ref[here : here + rows] = jnp.where(core == 0, high, low).astype(BF16)


def sums_third(core_ref, q_0, q_1, q_2, q_3, m_0, m_1, m_2, m_3, keep_ref, send_ref):
    q, m = sum_of((q_0, q_1, q_2, q_3)), sum_of((m_0, m_1, m_2, m_3))
    split_cores(core_ref[0], q, 24, 0, keep_ref, send_ref, 0)
    split_cores(core_ref[0], q, 8, 48, keep_ref, send_ref, 24)
    for k in range(2):
        split_cores(core_ref[0], m, 8, 16 * k, keep_ref, send_ref, 32 + 8 * k)


def cut_block(core, total_ref, keep_ref, send_ref):
    for rows, at, here in ((12, 0, 0), (4, 24, 12)):
        low, high = total_ref[at : at + rows, :], total_ref[at + rows : at + 2 * rows, :]
        keep_ref[here : here + rows, :] = jnp.where(core == 0, low, high)
        send_ref[here : here + rows, :] = jnp.where(core == 0, high, low).astype(BF16)


def sums_block(core_ref, parts_ref, keep_s, send_s, keep_f, send_f, total_ref):
    total = parts_ref[0].astype(F32)
    for i in range(1, 64):
        total = total + parts_ref[i].astype(F32)
    for rows, keep_ref, send_ref in ((slice(0, 32), keep_s, send_s), (slice(32, 64), keep_f, send_f)):
        total_ref[...] = total[rows]
        cut_block(core_ref[0], total_ref, keep_ref, send_ref)


def finish(
    core_ref, keep_t, got_t, keep_s, got_s, keep_f, got_f,
    first_qkv, first_out, second_qkv, second_out, merge, third_qkv, third_out,
    wide_ref,
):
    core = core_ref[0]

    def place(ref, keep, got, col):
        width = keep.shape[1]
        for block, side in ((keep, core), (got, 1 - core)):
            start = pl.multiple_of(side * ref.shape[1] // 2 + col, 128)
            ref[:, pl.ds(start, width)] = block

    place(third_qkv, keep_t[0:24, :], got_t[0:24, :].astype(F32), 0)
    place(third_out, keep_t[24:32, :], got_t[24:32, :].astype(F32), 0)
    place(merge, keep_t[32:40, :], got_t[32:40, :].astype(F32), 0)
    place(merge, keep_t[40:48, :], got_t[40:48, :].astype(F32), C2 // 2)
    for keep, got, qkv, out in ((keep_s, got_s, second_qkv, second_out), (keep_f, got_f, first_qkv, first_out)):
        wide_ref[...] = got[...].astype(F32)
        place(qkv, keep[0:12, :], wide_ref[0:12, :], 0)
        place(out, keep[12:16, :], wide_ref[12:16, :], 0)


SMEM = pl.BlockSpec(memory_space=pltpu.SMEM)
VMEM = pl.BlockSpec(memory_space=pltpu.VMEM)
HBM = pl.BlockSpec(memory_space=pltpu.HBM)
ANY = pl.BlockSpec(memory_space=pl.ANY)


class Loaded:
    def __init__(self, far, near, semaphore):
        self.near, self.waited = near, False
        self.copy = pltpu.make_async_copy(far, near, semaphore)
        self.copy.start()

    def ready(self):
        if not self.waited:
            self.copy.wait()
            self.waited = True
        return self.near

    def __getitem__(self, where):
        return self.ready()[where]


class Stored:
    def __init__(self, far, near, semaphore):
        self.far, self.near, self.semaphore, self.copy = far, near, semaphore, None

    def send(self):
        if self.copy is None:
            self.copy = pltpu.make_async_copy(self.near, self.far, self.semaphore)
            self.copy.start()

    @property
    def shape(self):
        return self.near.shape

    @property
    def at(self):
        return self.near.at

    def __getitem__(self, where):
        return self.near[where]

    def __setitem__(self, where, value):
        self.near[where] = value


class Far:
    def __init__(self, what):
        self.what = what


def call(kernel, us, scalars, arrays, outs, scratch=(), limit=24):
    far_in = [isinstance(a, Far) for a in arrays]
    far_out = [isinstance(o, Far) for o in outs]
    arrays = [a.what if f else a for a, f in zip(arrays, far_in)]
    outs = [o.what if f else o for o, f in zip(outs, far_out)]
    outs = [o if isinstance(o, jax.ShapeDtypeStruct) else jax.ShapeDtypeStruct(o, BF16) for o in outs]
    staged_in = [a for a, f in zip(arrays, far_in) if f]
    staged_out = [o for o, f in zip(outs, far_out) if f]

    def body(*refs):
        refs = list(refs)
        take = lambda count: [refs.pop(0) for _ in range(count)]
        numbers, given, made = take(len(scalars)), take(len(arrays)), take(len(outs))
        near_in, near_out, own = take(len(staged_in)), take(len(staged_out)), take(len(scratch))
        in_sem, out_sem = refs
        count = 0
        for i, far in enumerate(far_in):
            if far:
                given[i] = Loaded(given[i], near_in[count], in_sem.at[count])
                count += 1
        count = 0
        for i, far in enumerate(far_out):
            if far:
                made[i] = Stored(made[i], near_out[count], out_sem.at[count])
                count += 1
        kernel(*numbers, *given, *made, *own)
        for ref in given:
            if isinstance(ref, Loaded):
                ref.ready()
        send(*made)
        for ref in made:
            if isinstance(ref, Stored):
                ref.copy.wait()

    return pl.pallas_call(
        body,
        name=kernel.__name__,
        out_shape=outs,
        in_specs=[SMEM] * len(scalars) + [HBM if f else VMEM for f in far_in],
        out_specs=[HBM if f else VMEM for f in far_out],
        scratch_shapes=[pltpu.VMEM(a.shape, a.dtype) for a in staged_in + staged_out]
        + [pltpu.VMEM(s, d) for s, d in scratch]
        + [pltpu.SemaphoreType.DMA((max(1, len(staged_in)),)), pltpu.SemaphoreType.DMA((max(1, len(staged_out)),))],
        cost_estimate=pl.CostEstimate(flops=int(us * 1.15e10), bytes_accessed=0, transcendentals=0),
        compiler_params=pltpu.CompilerParams(vmem_limit_bytes=limit * 2**20),
    )(*scalars, *arrays)


def after(block, *others):
    def nothing(*refs):
        pass

    return pl.pallas_call(
        nothing,
        cost_estimate=pl.CostEstimate(flops=1, bytes_accessed=0, transcendentals=0),
        name="after",
        out_shape=jax.ShapeDtypeStruct(block.shape, block.dtype),
        in_specs=[ANY] * (1 + len(others)),
        out_specs=ANY,
        input_output_aliases={0: 0},
    )(block, *others)


def send_strips(strips, step):
    lats, lons = 8, 16

    def route(lat_step, lon_step):
        return [
            (a * lons + o, (a + lat_step) % lats * lons + (o + lon_step) % lons)
            for a in range(lats)
            for o in range(lons)
        ]

    steps = ((step, 0), (0, step), (step, step))
    return [lax.ppermute(s, EVERY, route(*r)) for s, r in zip(strips, steps)]


def other_core(block):
    return lax.ppermute(block, "c", [(0, 1), (1, 0)])


def scatter(block, axis):
    return lax.psum_scatter(block, axis, scatter_dimension=0, tiled=True)


def to_chips(block):
    return lax.all_to_all(block, CHIPS, split_axis=0, concat_axis=0, tiled=True)


def onward(pieces, axis):
    moved = [
        lax.ppermute(piece, axis, [(i, (i + d) % 4) for i in range(4)])
        for d, piece in enumerate(pieces)
        if d > 0
    ]
    return [pieces[0], *moved]


def index(axes):
    return lax.axis_index(axes).astype(jnp.int32).reshape(1)


def on_device(
    tokens, qkv_first, out_first, qkv_second, out_second, merge_weight, qkv_third, out_third, cotangent
):
    pack, keep, place, patch = (Far(jnp.asarray(m)) for m in routing())
    core = index("c")
    last = (index(LAT) == 7).astype(jnp.int32)
    tok = tokens.reshape(TOK, C1)
    wide, slim = (TOK, 3 * C1), (TOK, C1)
    strip_shapes = [(STRIP_A, C1), (STRIP_B, C1), (STRIP_D, C1)]
    probs = (2, C1 // PAIR, 2 * BAND, BAND)
    one, sa, sb, sd, qkv1, o1, p1 = call(
        first_forward, 5, [], [Far(tok), Far(qkv_first), Far(out_first), pack],
        [Far(slim), *map(Far, strip_shapes), Far(wide), Far(slim), Far(probs)], limit=56,
    )
    arrived = send_strips((sa, sb, sd), -1)
    rolled, own, sa, sb, sd, qkv2, o2, p2 = call(
        second_forward, 6, [last], [Far(one), *map(Far, arrived), Far(qkv_second), Far(out_second), keep, place],
        [Far(slim), Far(slim), *map(Far, strip_shapes), Far(wide), Far(slim), Far(probs)], limit=40,
    )
    arrived = send_strips((sa, sb, sd), 1)
    latent, two_cot, sa, sb, sd, acts = call(
        third_both, 18, [],
        [one, own, *arrived, Far(cotangent[0]), merge_weight, qkv_third, out_third, pack, patch],
        [Far((M_ROWS, M_COLS, C2)), slim, *strip_shapes, (M_PAD, A_ALL)],
        [((M_PAD, C2), F32), ((M_PAD, 3 * C2), BF16), ((M_PAD, C2), BF16), ((1, C2 // PAIR, 2 * M_PAD, M_PAD), BF16)],
    )
    acts_got = other_core(acts)
    arrived = send_strips((sa, sb, sd), -1)
    half_t = C2 // 2
    (grads_q,) = call(attention_grads, 4, [core], [acts, acts_got], [(64, 64, half_t)])
    part_q = scatter(grads_q, "x")
    own, sa, sb, sd, dqkv2, unit2, cot2 = call(
        second_back, 10, [],
        [Far(two_cot), *map(Far, arrived), Far(after(rolled, grads_q)), Far(qkv2), Far(p2), Far(qkv_second), Far(out_second), keep, place],
        [Far(slim), *map(Far, strip_shapes), Far(wide), Far(slim), Far(slim)], [(slim, BF16)], limit=56,
    )
    arrived = send_strips((sa, sb, sd), 1)
    half = (64, 32, C1 // 2)
    keep2, send2 = call(block_grads, 4, [core], [Far(dqkv2), Far(unit2), Far(cot2), Far(o2)], [Far(half), Far(half)], limit=56)
    got2 = other_core(send2)
    piece = (16, 32, half_t)
    m = call(
        merge_grads, 4, [core, index("y")], [after(acts, own), acts_got], [piece] * 4, [((4, *piece), BF16)]
    )
    cot1, dqkv1, keep1, send1 = call(
        first_back, 9, [core], [Far(two_cot), Far(after(own, keep2, m[0])), *map(Far, arrived), Far(tok), Far(qkv1), Far(p1), Far(o1), Far(out_first), pack],
        [Far(slim), Far(wide), Far(half), Far(half)], [(slim, BF16), (slim, BF16)], limit=56,
    )
    got1 = other_core(send1)
    m = onward(m, "y")
    (tokens_grad,) = call(first_input, 4, [], [cot1, dqkv1, Far(tok), qkv_first], [slim])
    (pairs,) = call(pack_pairs, 0.001, [], [keep2, got2, after(keep1, tokens_grad), got1], [(64, 64, C1 // 2)])
    q_piece, m_piece = (4, 64, half_t), (4, 32, half_t)
    parts = call(
        second_pieces, 3, [index(DEPTH), index("x")], [after(part_q.reshape(4, *q_piece), pairs), *m],
        [q_piece] * 4 + [m_piece] * 4, [((4, *m_piece), BF16)],
    )
    q, m = onward(parts[:4], DEPTH), onward(parts[4:], "x")
    swapped = to_chips(after(pairs, parts[0]))
    parts = call(
        last_pieces, 2, [index("y"), index(DEPTH)], [*q, *m], [q_piece[1:]] * 4 + [m_piece[1:]] * 4,
        [(q_piece, BF16), (m_piece, BF16)],
    )
    q, m = onward(parts[:4], "y"), onward(parts[4:], DEPTH)

    def halves(rows, width):
        return [jax.ShapeDtypeStruct((rows, width), F32), jax.ShapeDtypeStruct((rows, width), BF16)]

    total = [((32, 256), F32)]
    keep_s, send_s, keep_f, send_f = call(sums_block, 2, [core], [swapped], halves(16, 256) * 2, total)
    keep_t, send_t = call(sums_third, 0.001, [core], [*q, *m], halves(48, half_t))
    sizes = [(12, C1), (4, C1), (12, C1), (4, C1), (8, 2 * C2), (24, C2), (8, C2)]
    grads = call(
        finish, 2, [core],
        [keep_t, other_core(send_t), keep_s, other_core(send_s), keep_f, other_core(send_f)],
        [jax.ShapeDtypeStruct(s, F32) for s in sizes], [((16, 256), F32)],
    )
    return (latent[None], tokens_grad.reshape(tokens.shape), *grads)


def solution(mesh):
    split = Mesh(mesh.devices.reshape(4, 2, 2, 4, 2), EVERY)
    grid = P(None, LAT, LON, None)
    return jax.shard_map(
        on_device,
        mesh=split,
        in_specs=(grid,) + (P(),) * 7 + (grid,),
        out_specs=(grid, grid) + (P(EVERY, None),) * 7,
        check_vma=False,
    )
```

```python
import jax
import jax.numpy as jnp
import numpy as np
from jax import lax
from jax.experimental import pallas as pl
from jax.experimental.pallas import tpu as pltpu
from jax.sharding import Mesh, PartitionSpec as P

F32 = jnp.float32
BF16 = jnp.bfloat16
HDIM = 64
PAIR = 2 * HDIM
SCALE = HDIM ** (-0.5)
WA = 6
WO = 12
ROWS = 12
COLS = 24
TOK = ROWS * COLS
BAND = WA * COLS
C1 = 512
C2 = 1024
M_ROWS = 6
M_COLS = 12
M_TOK = M_ROWS * M_COLS
M_PAD = 80
STRIP_A = 64
STRIP_B = 64
STRIP_D = 32
STRIPS = STRIP_A + STRIP_B + STRIP_D
EPSILON = 1e-05
FAR = -1e30

NN = (((1,), (0,)), ((), ()))
NT = (((1,), (1,)), ((), ()))
TN = (((0,), (0,)), ((), ()))

LAT = ("x", "zh")
LON = ("zl", "y", "c")
DEPTH = ("zh", "zl")
CHIPS = ("x", "zh", "zl", "y")
EVERY = ("x", "zh", "zl", "y", "c")

A_CT = 0
A_O = A_CT + C2
A_DT = A_O + C2
A_N = A_DT + 3 * C2
A_HC = A_N + C2
A_NM = A_HC + C2
A_ALL = A_NM + 2 * C2


def routing():
    pack = np.zeros((STRIPS, TOK), np.float32)
    keep = np.zeros((TOK, TOK), np.float32)
    place = np.zeros((TOK, STRIPS), np.float32)
    half_a, half_o = WA // 2, WO // 2
    count = {"a": 0, "b": STRIP_A, "d": STRIP_A + STRIP_B}
    for r in range(ROWS):
        for c in range(COLS):
            gr, gc = r + half_a, c + half_o
            src = (gr % ROWS) * COLS + gc % COLS
            dst = r * COLS + c
            if gr < ROWS and gc < COLS:
                keep[dst, src] = 1
                continue
            kind = "a" if gc < COLS else ("b" if gr < ROWS else "d")
            slot = count[kind]
            count[kind] += 1
            pack[slot, src] = 1
            place[dst, slot] = 1
    patch = np.zeros((4 * M_PAD, TOK), np.float32)
    for part in range(4):
        for i in range(M_ROWS):
            for j in range(M_COLS):
                src = (2 * i + part % 2) * COLS + 2 * j + part // 2
                patch[part * M_PAD + i * M_COLS + j, src] = 1
    return [m.astype(jnp.bfloat16) for m in (pack, keep, place, patch)]


def dot(a, b, dims):
    return lax.dot_general(a, b, dims, preferred_element_type=F32)


def norm(field):
    values = field.astype(F32)
    centered = values - jnp.mean(values, axis=-1, keepdims=True)
    inverse = lax.rsqrt(jnp.mean(centered * centered, axis=-1, keepdims=True) + EPSILON)
    return centered * inverse, inverse


def norm_back(cotan, unit, inverse):
    cotan = cotan.astype(F32)
    along = jnp.mean(cotan * unit, axis=-1, keepdims=True)
    return (inverse * (cotan - jnp.mean(cotan, axis=-1, keepdims=True) - unit * along)).astype(BF16)


def add(a, b):
    return (a.astype(F32) + b.astype(F32)).astype(BF16)


def stacked(block):
    lane = lax.broadcasted_iota(jnp.int32, (1, PAIR), 1)
    first = jnp.where(lane < HDIM, 1.0, 0.0).astype(BF16)
    second = jnp.where(lane < HDIM, 0.0, 1.0).astype(BF16)
    return jnp.concatenate([block * first, block * second], axis=0)


def joined(both):
    size = both.shape[0] // 2
    lane = lax.broadcasted_iota(jnp.int32, (size, PAIR), 1)
    return jnp.where(lane < HDIM, both[:size], both[size:])


def softmax(queries, keys, bias):
    scores = dot(queries, keys, NT) * SCALE + bias
    raised = jnp.exp(scores - jnp.max(scores, axis=-1, keepdims=True))
    return raised * (1.0 / jnp.sum(raised, axis=-1, keepdims=True))


def attend(qkv_ref, o_ref, p_ref, channels, spans, biases):
    for n, ((start, size), bias) in enumerate(zip(spans, biases)):
        rows = pl.ds(start, size)
        for pair in range(channels // PAIR):
            lanes = pair * PAIR
            q = stacked(qkv_ref[rows, lanes : lanes + PAIR])
            k = qkv_ref[rows, channels + lanes : channels + lanes + PAIR]
            v = qkv_ref[rows, 2 * channels + lanes : 2 * channels + lanes + PAIR]
            p = softmax(q, k, bias).astype(BF16)
            p_ref[n, pair] = p
            o_ref[rows, lanes : lanes + PAIR] = joined(dot(p, v, NN)).astype(BF16)


def attend_back(qkv_ref, p_ref, do_ref, dqkv_ref, channels, spans):
    for n, (start, size) in enumerate(spans):
        rows = pl.ds(start, size)
        for pair in range(channels // PAIR):
            lanes = pair * PAIR
            q = stacked(qkv_ref[rows, lanes : lanes + PAIR])
            k = qkv_ref[rows, channels + lanes : channels + lanes + PAIR]
            v = qkv_ref[rows, 2 * channels + lanes : 2 * channels + lanes + PAIR]
            do = stacked(do_ref[rows, lanes : lanes + PAIR])
            p = p_ref[n, pair].astype(F32)
            dp = dot(do, v, NT)
            inner = jnp.sum(p * dp, axis=-1, keepdims=True)
            ds = (p * (dp - inner) * SCALE).astype(BF16)
            dq = joined(dot(ds, k, NN))
            dk = dot(ds, q, TN)
            dv = dot(p_ref[n, pair], do, TN)
            dqkv_ref[rows, lanes : lanes + PAIR] = dq.astype(BF16)
            dqkv_ref[rows, channels + lanes : channels + lanes + PAIR] = dk.astype(BF16)
            dqkv_ref[rows, 2 * channels + lanes : 2 * channels + lanes + PAIR] = dv.astype(BF16)


BANDS = [(0, BAND), (BAND, BAND)]


def band_biases(last_lat):
    def ids(dim, shape):
        token = lax.broadcasted_iota(jnp.int32, shape, dim)
        row = (token * 171) >> 12
        col = token - COLS * row
        return jnp.where(col >= WO, 1.0, 0.0), jnp.where(row >= WA // 2, 2.0, 0.0)

    win_q, half_q = ids(0, (BAND, BAND))
    win_k, half_k = ids(1, (BAND, BAND))
    plain = jnp.where(win_q == win_k, 0.0, FAR)
    plain = jnp.concatenate([plain, plain], axis=0)
    if last_lat is None:
        return [plain, plain]
    cut = jnp.where(win_q + half_q == win_k + half_k, 0.0, FAR)
    cut = jnp.concatenate([cut, cut], axis=0)
    return [plain, jnp.where(last_lat == 1, cut, plain)]


def put_strips(refs, strips):
    bounds = (0, STRIP_A, STRIP_A + STRIP_B, STRIPS)
    for ref, low, high in zip(refs, bounds[:-1], bounds[1:]):
        ref[...] = strips[low:high].astype(BF16)
        send(ref)


def send(*refs):
    for ref in refs:
        if isinstance(ref, Stored):
            ref.send()


def get_strips(refs):
    return jnp.concatenate([ref[...] for ref in refs], axis=0)


def first_forward(tok_ref, wqkv_ref, wo_ref, pack_ref, one_ref, out_a, out_b, out_d, qkv_ref, o_ref, p_ref):
    unit, _ = norm(tok_ref[...])
    qkv_ref[...] = dot(unit.astype(BF16), wqkv_ref[...], NT).astype(BF16)
    send(qkv_ref)
    attend(qkv_ref, o_ref, p_ref, C1, BANDS, band_biases(None))
    send(p_ref, o_ref)
    out = dot(o_ref[...], wo_ref[...], NT).astype(BF16)
    one = add(tok_ref[...], out)
    one_ref[...] = one
    put_strips((out_a, out_b, out_d), dot(pack_ref[...], one, NN))


def second_forward(
    last_ref, one_ref, in_a, in_b, in_d, wqkv_ref, wo_ref, keep_ref, place_ref,
    rolled_ref, own_ref, out_a, out_b, out_d, qkv_ref, o_ref, p_ref,
):
    arrived = get_strips((in_a, in_b, in_d))
    rolled = (dot(keep_ref[...], one_ref[...], NN) + dot(place_ref[...], arrived, NN)).astype(BF16)
    rolled_ref[...] = rolled
    unit, _ = norm(rolled)
    qkv_ref[...] = dot(unit.astype(BF16), wqkv_ref[...], NT).astype(BF16)
    send(qkv_ref, rolled_ref)
    attend(qkv_ref, o_ref, p_ref, C1, BANDS, band_biases(last_ref[0]))
    send(p_ref, o_ref)
    out = dot(o_ref[...], wo_ref[...], NT).astype(BF16)
    put_strips((out_a, out_b, out_d), dot(place_ref[...], out, TN))
    own_ref[...] = dot(keep_ref[...], out, TN).astype(BF16)


def third_both(
    one_ref, own_ref, in_a, in_b, in_d, ct_ref, wm_ref, wqkv_ref, wo_ref, pack_ref, patch_ref,
    latent_ref, two_cot_ref, out_a, out_b, out_d, acts_ref,
    wide, qkv_ref, do_ref, p_ref,
):
    arrived = get_strips((in_a, in_b, in_d))
    out_two = own_ref[...].astype(F32) + dot(pack_ref[...], arrived, TN)
    two = (one_ref[...].astype(F32) + out_two).astype(BF16)
    parts = dot(patch_ref[...], two, NN)
    merged = jnp.concatenate([parts[p * M_PAD : (p + 1) * M_PAD] for p in range(4)], axis=1)
    unit_m, inverse_m = norm(merged)
    acts_ref[:, A_NM : A_NM + 2 * C2] = unit_m.astype(BF16)
    hidden = dot(acts_ref[:, A_NM : A_NM + 2 * C2], wm_ref[...], NT).astype(BF16)
    unit_h, inverse_h = norm(hidden)
    acts_ref[:, A_N : A_N + C2] = unit_h.astype(BF16)
    qkv_ref[...] = dot(acts_ref[:, A_N : A_N + C2], wqkv_ref[...], NT).astype(BF16)
    key = lax.broadcasted_iota(jnp.int32, (2 * M_PAD, M_PAD), 1)
    bias = jnp.where(key < M_TOK, 0.0, FAR)
    span = [(0, M_PAD)]
    attend(qkv_ref, acts_ref.at[:, A_O : A_O + C2], p_ref, C2, span, [bias])
    out = dot(acts_ref[:, A_O : A_O + C2], wo_ref[...], NT).astype(BF16)
    wide[...] = hidden.astype(F32) + out.astype(F32)
    for i in range(M_ROWS):
        latent_ref[i] = wide[i * M_COLS : (i + 1) * M_COLS, :].astype(BF16)
    send(latent_ref)
    wide[M_TOK:, :] = jnp.zeros((M_PAD - M_TOK, C2), F32)
    for i in range(M_ROWS):
        wide[i * M_COLS : (i + 1) * M_COLS, :] = ct_ref[i].astype(F32)
    cot = wide[...].astype(BF16)
    acts_ref[:, A_CT : A_CT + C2] = cot
    do_ref[...] = dot(cot, wo_ref[...], NN).astype(BF16)
    attend_back(qkv_ref, p_ref, do_ref, acts_ref.at[:, A_DT : A_DT + 3 * C2], C2, span)
    dn = dot(acts_ref[:, A_DT : A_DT + 3 * C2], wqkv_ref[...], NN).astype(BF16)
    hidden_cot = add(cot, norm_back(dn, unit_h, inverse_h))
    acts_ref[:, A_HC : A_HC + C2] = hidden_cot
    send(acts_ref)
    dnm = dot(hidden_cot, wm_ref[...], NN).astype(BF16)
    merged_cot = norm_back(dnm, unit_m, inverse_m)
    two_cot = dot(patch_ref[0:M_PAD, :], merged_cot[:, 0:C1], TN)
    for p in range(1, 4):
        two_cot = two_cot + dot(
            patch_ref[p * M_PAD : (p + 1) * M_PAD, :], merged_cot[:, p * C1 : (p + 1) * C1], TN
        )
    two_cot = two_cot.astype(BF16)
    two_cot_ref[...] = two_cot
    send(two_cot_ref)
    put_strips((out_a, out_b, out_d), dot(pack_ref[...], two_cot, NN))


def both_cores(mine_ref, other_ref, start, width):
    where = pl.ds(start, width)
    return jnp.concatenate([mine_ref[:, where], other_ref[:, where]], axis=0)


def attention_grads(core_ref, mine_ref, other_ref, out_ref):
    half = C2 // 2
    n = both_cores(mine_ref, other_ref, pl.multiple_of(A_N + core_ref[0] * half, half), half)
    o = both_cores(mine_ref, other_ref, pl.multiple_of(A_O + core_ref[0] * half, half), half)
    for piece in range(8):
        step = 3 * C2 // 8
        grad = dot(both_cores(mine_ref, other_ref, A_DT + piece * step, step), n, TN).astype(BF16)
        out_ref[piece * 8 : piece * 8 + 8, 0:48] = grad.reshape(8, 48, half)
    for piece in range(4):
        step = C2 // 4
        grad = dot(both_cores(mine_ref, other_ref, A_CT + piece * step, step), o, TN).astype(BF16)
        out_ref[piece * 16 : piece * 16 + 16, 48:64] = grad.reshape(16, 16, half)


def merge_grads(core_ref, y_ref, mine_ref, other_ref, out_0, out_1, out_2, out_3, all_ref):
    half = C2 // 2
    nm = both_cores(mine_ref, other_ref, pl.multiple_of(A_NM + core_ref[0] * C2, C2), C2)
    for piece in range(4):
        step = C2 // 4
        hc = both_cores(mine_ref, other_ref, A_HC + piece * step, step)
        for side in range(2):
            grad = dot(hc, nm[:, side * half : side * half + half], TN).astype(BF16).reshape(4, 4, 16, half)
            for y in range(4):
                all_ref[y, piece * 4 : piece * 4 + 4, 16 * side : 16 * side + 16] = grad[:, y]
    for d, ref in enumerate((out_0, out_1, out_2, out_3)):
        ref[...] = all_ref[(y_ref[0] + d) % 4]


def sum_of(refs):
    total = refs[0][...].astype(F32)
    for ref in refs[1:]:
        total = total + ref[...].astype(F32)
    return total


def second_pieces(z_ref, x_ref, q_ref, m_0, m_1, m_2, m_3, q_out0, q_out1, q_out2, q_out3, o_0, o_1, o_2, o_3, m_ref):
    m_ref[...] = sum_of((m_0, m_1, m_2, m_3)).astype(BF16).reshape(4, 4, 32, C2 // 2)
    for d, (q, m) in enumerate(zip((q_out0, q_out1, q_out2, q_out3), (o_0, o_1, o_2, o_3))):
        q[...] = q_ref[(z_ref[0] + d) % 4]
        m[...] = m_ref[(x_ref[0] + d) % 4]


def last_pieces(
    y_ref, z_ref, q_0, q_1, q_2, q_3, m_0, m_1, m_2, m_3, p_0, p_1, p_2, p_3, o_0, o_1, o_2, o_3, q_ref, m_ref
):
    q_ref[...] = sum_of((q_0, q_1, q_2, q_3)).astype(BF16)
    m_ref[...] = sum_of((m_0, m_1, m_2, m_3)).astype(BF16)
    for d, (q, m) in enumerate(zip((p_0, p_1, p_2, p_3), (o_0, o_1, o_2, o_3))):
        q[...] = q_ref[(y_ref[0] + d) % 4]
        m[...] = m_ref[(z_ref[0] + d) % 4]


def pack_pairs(mine_s, other_s, mine_f, other_f, out_ref):
    out_ref[:, 0:32] = add(mine_s[...], other_s[...])
    out_ref[:, 32:64] = add(mine_f[...], other_f[...])


def block_grads(core_ref, dqkv_ref, unit_ref, cot_ref, o_ref, keep_out, send_out):
    half = C1 // 2
    for ref, side in ((send_out, 1 - core_ref[0]), (keep_out, core_ref[0])):
        where = pl.ds(pl.multiple_of(side * half, half), half)
        grad_qkv = dot(dqkv_ref[...], unit_ref[:, where], TN).reshape(64, 24, half)
        grad_out = dot(cot_ref[...], o_ref[:, where], TN).reshape(64, 8, half)
        ref[...] = jnp.concatenate([grad_qkv, grad_out], axis=1).astype(BF16)
        send(ref)


def second_back(
    two_cot_ref, in_a, in_b, in_d, rolled_ref, qkv_ref, p_ref, wqkv_ref, wo_ref, keep_ref, place_ref,
    own_ref, out_a, out_b, out_d, dqkv_ref, unit_ref, cot_ref,
    do_ref,
):
    arrived = get_strips((in_a, in_b, in_d))
    cot = (dot(keep_ref[...], two_cot_ref[...], NN) + dot(place_ref[...], arrived, NN)).astype(BF16)
    cot_ref[...] = cot
    unit, inverse = norm(rolled_ref[...])
    unit_ref[...] = unit.astype(BF16)
    do_ref[...] = dot(cot, wo_ref[...], NN).astype(BF16)
    attend_back(qkv_ref, p_ref, do_ref, dqkv_ref, C1, BANDS)
    send(unit_ref, cot_ref, dqkv_ref)
    dn = dot(dqkv_ref[...], wqkv_ref[...], NN).astype(BF16)
    rolled_cot = norm_back(dn, unit, inverse)
    put_strips((out_a, out_b, out_d), dot(place_ref[...], rolled_cot, TN))
    own_ref[...] = dot(keep_ref[...], rolled_cot, TN).astype(BF16)


def first_back(
    core_ref, two_cot_ref, own_ref, in_a, in_b, in_d, tok_ref, qkv_ref, p_ref, o_ref, wo_ref, pack_ref,
    cot_ref, dqkv_ref, grad_keep, grad_send,
    do_ref, unit_ref,
):
    arrived = get_strips((in_a, in_b, in_d))
    back = own_ref[...].astype(F32) + dot(pack_ref[...], arrived, TN)
    cot = (two_cot_ref[...].astype(F32) + back).astype(BF16)
    cot_ref[...] = cot
    unit_ref[...] = norm(tok_ref[...])[0].astype(BF16)
    do_ref[...] = dot(cot, wo_ref[...], NN).astype(BF16)
    attend_back(qkv_ref, p_ref, do_ref, dqkv_ref, C1, BANDS)
    send(cot_ref, dqkv_ref)
    block_grads(core_ref, dqkv_ref, unit_ref, cot_ref, o_ref, grad_keep, grad_send)


def first_input(cot_ref, dqkv_ref, tok_ref, wqkv_ref, grad_ref):
    unit, inverse = norm(tok_ref[...])
    dn = dot(dqkv_ref[...], wqkv_ref[...], NN).astype(BF16)
    grad_ref[...] = add(cot_ref[...], norm_back(dn, unit, inverse))


def split_cores(core, total, rows, at, keep_ref, send_ref, here):
    low, high = total[at : at + rows], total[at + rows : at + 2 * rows]
    keep_ref[here : here + rows] = jnp.where(core == 0, low, high)
    send_ref[here : here + rows] = jnp.where(core == 0, high, low).astype(BF16)


def sums_third(core_ref, q_0, q_1, q_2, q_3, m_0, m_1, m_2, m_3, keep_ref, send_ref):
    q, m = sum_of((q_0, q_1, q_2, q_3)), sum_of((m_0, m_1, m_2, m_3))
    split_cores(core_ref[0], q, 24, 0, keep_ref, send_ref, 0)
    split_cores(core_ref[0], q, 8, 48, keep_ref, send_ref, 24)
    for k in range(2):
        split_cores(core_ref[0], m, 8, 16 * k, keep_ref, send_ref, 32 + 8 * k)


def cut_block(core, total_ref, keep_ref, send_ref):
    for rows, at, here in ((12, 0, 0), (4, 24, 12)):
        low, high = total_ref[at : at + rows, :], total_ref[at + rows : at + 2 * rows, :]
        keep_ref[here : here + rows, :] = jnp.where(core == 0, low, high)
        send_ref[here : here + rows, :] = jnp.where(core == 0, high, low).astype(BF16)


def sums_block(core_ref, parts_ref, keep_s, send_s, keep_f, send_f, total_ref):
    total = parts_ref[0].astype(F32)
    for i in range(1, 64):
        total = total + parts_ref[i].astype(F32)
    for rows, keep_ref, send_ref in ((slice(0, 32), keep_s, send_s), (slice(32, 64), keep_f, send_f)):
        total_ref[...] = total[rows]
        cut_block(core_ref[0], total_ref, keep_ref, send_ref)


def finish(
    core_ref, keep_t, got_t, keep_s, got_s, keep_f, got_f,
    first_qkv, first_out, second_qkv, second_out, merge, third_qkv, third_out,
    wide_ref,
):
    core = core_ref[0]

    def place(ref, keep, got, col):
        width = keep.shape[1]
        for block, side in ((keep, core), (got, 1 - core)):
            start = pl.multiple_of(side * ref.shape[1] // 2 + col, 128)
            ref[:, pl.ds(start, width)] = block

    place(third_qkv, keep_t[0:24, :], got_t[0:24, :].astype(F32), 0)
    place(third_out, keep_t[24:32, :], got_t[24:32, :].astype(F32), 0)
    place(merge, keep_t[32:40, :], got_t[32:40, :].astype(F32), 0)
    place(merge, keep_t[40:48, :], got_t[40:48, :].astype(F32), C2 // 2)
    for keep, got, qkv, out in ((keep_s, got_s, second_qkv, second_out), (keep_f, got_f, first_qkv, first_out)):
        wide_ref[...] = got[...].astype(F32)
        place(qkv, keep[0:12, :], wide_ref[0:12, :], 0)
        place(out, keep[12:16, :], wide_ref[12:16, :], 0)


SMEM = pl.BlockSpec(memory_space=pltpu.SMEM)
VMEM = pl.BlockSpec(memory_space=pltpu.VMEM)
HBM = pl.BlockSpec(memory_space=pltpu.HBM)
ANY = pl.BlockSpec(memory_space=pl.ANY)


class Loaded:
    def __init__(self, far, near, semaphore):
        self.near, self.waited = near, False
        self.copy = pltpu.make_async_copy(far, near, semaphore)
        self.copy.start()

    def ready(self):
        if not self.waited:
            self.copy.wait()
            self.waited = True
        return self.near

    def __getitem__(self, where):
        return self.ready()[where]


class Stored:
    def __init__(self, far, near, semaphore):
        self.far, self.near, self.semaphore, self.copy = far, near, semaphore, None

    def send(self):
        if self.copy is None:
            self.copy = pltpu.make_async_copy(self.near, self.far, self.semaphore)
            self.copy.start()

    @property
    def shape(self):
        return self.near.shape

    @property
    def at(self):
        return self.near.at

    def __getitem__(self, where):
        return self.near[where]

    def __setitem__(self, where, value):
        self.near[where] = value


class Far:
    def __init__(self, what):
        self.what = what


def call(kernel, us, scalars, arrays, outs, scratch=(), limit=24, order=None):
    far_in = [isinstance(a, Far) for a in arrays]
    far_out = [isinstance(o, Far) for o in outs]
    arrays = [a.what if f else a for a, f in zip(arrays, far_in)]
    outs = [o.what if f else o for o, f in zip(outs, far_out)]
    outs = [o if isinstance(o, jax.ShapeDtypeStruct) else jax.ShapeDtypeStruct(o, BF16) for o in outs]
    staged_in = [a for a, f in zip(arrays, far_in) if f]
    staged_out = [o for o, f in zip(outs, far_out) if f]

    def body(*refs):
        refs = list(refs)
        take = lambda count: [refs.pop(0) for _ in range(count)]
        numbers, given, made = take(len(scalars)), take(len(arrays)), take(len(outs))
        near_in, near_out, own = take(len(staged_in)), take(len(staged_out)), take(len(scratch))
        in_sem, out_sem = refs
        count = 0
        slots = [i for i, far in enumerate(far_in) if far]
        for i in order or slots:
            count = slots.index(i)
            given[i] = Loaded(given[i], near_in[count], in_sem.at[count])
        count = 0
        for i, far in enumerate(far_out):
            if far:
                made[i] = Stored(made[i], near_out[count], out_sem.at[count])
                count += 1
        kernel(*numbers, *given, *made, *own)
        for ref in given:
            if isinstance(ref, Loaded):
                ref.ready()
        send(*made)
        for ref in made:
            if isinstance(ref, Stored):
                ref.copy.wait()

    return pl.pallas_call(
        body,
        name=kernel.__name__,
        out_shape=outs,
        in_specs=[SMEM] * len(scalars) + [HBM if f else VMEM for f in far_in],
        out_specs=[HBM if f else VMEM for f in far_out],
        scratch_shapes=[pltpu.VMEM(a.shape, a.dtype) for a in staged_in + staged_out]
        + [pltpu.VMEM(s, d) for s, d in scratch]
        + [pltpu.SemaphoreType.DMA((max(1, len(staged_in)),)), pltpu.SemaphoreType.DMA((max(1, len(staged_out)),))],
        cost_estimate=pl.CostEstimate(flops=int(us * 1.15e10), bytes_accessed=0, transcendentals=0),
        compiler_params=pltpu.CompilerParams(vmem_limit_bytes=limit * 2**20),
    )(*scalars, *arrays)


def after(block, *others):
    def nothing(*refs):
        pass

    return pl.pallas_call(
        nothing,
        cost_estimate=pl.CostEstimate(flops=1, bytes_accessed=0, transcendentals=0),
        name="after",
        out_shape=jax.ShapeDtypeStruct(block.shape, block.dtype),
        in_specs=[ANY] * (1 + len(others)),
        out_specs=ANY,
        input_output_aliases={0: 0},
    )(block, *others)


def send_strips(strips, step):
    lats, lons = 8, 16

    def route(lat_step, lon_step):
        return [
            (a * lons + o, (a + lat_step) % lats * lons + (o + lon_step) % lons)
            for a in range(lats)
            for o in range(lons)
        ]

    steps = ((step, 0), (0, step), (step, step))
    return [lax.ppermute(s, EVERY, route(*r)) for s, r in zip(strips, steps)]


def other_core(block):
    return lax.ppermute(block, "c", [(0, 1), (1, 0)])


def scatter(block, axis):
    return lax.psum_scatter(block, axis, scatter_dimension=0, tiled=True)


def to_chips(block):
    return lax.all_to_all(block, CHIPS, split_axis=0, concat_axis=0, tiled=True)


def onward(pieces, axis):
    moved = [
        lax.ppermute(piece, axis, [(i, (i + d) % 4) for i in range(4)])
        for d, piece in enumerate(pieces)
        if d > 0
    ]
    return [pieces[0], *moved]


def index(axes):
    return lax.axis_index(axes).astype(jnp.int32).reshape(1)


def on_device(
    tokens, qkv_first, out_first, qkv_second, out_second, merge_weight, qkv_third, out_third, cotangent
):
    pack, keep, place, patch = (Far(jnp.asarray(m)) for m in routing())
    core = index("c")
    last = (index(LAT) == 7).astype(jnp.int32)
    tok = tokens.reshape(TOK, C1)
    wide, slim = (TOK, 3 * C1), (TOK, C1)
    strip_shapes = [(STRIP_A, C1), (STRIP_B, C1), (STRIP_D, C1)]
    probs = (2, C1 // PAIR, 2 * BAND, BAND)
    one, sa, sb, sd, qkv1, o1, p1 = call(
        first_forward, 5, [], [Far(tok), Far(qkv_first), Far(out_first), pack],
        [Far(slim), *map(Far, strip_shapes), Far(wide), Far(slim), Far(probs)], limit=56,
    )
    arrived = send_strips((sa, sb, sd), -1)
    rolled, own, sa, sb, sd, qkv2, o2, p2 = call(
        second_forward, 6, [last], [Far(one), *map(Far, arrived), Far(qkv_second), Far(out_second), keep, place],
        [Far(slim), Far(slim), *map(Far, strip_shapes), Far(wide), Far(slim), Far(probs)], limit=40,
        order=(6, 7, 0, 1, 2, 3, 4, 5),
    )
    arrived = send_strips((sa, sb, sd), 1)
    latent, two_cot, sa, sb, sd, acts = call(
        third_both, 18, [],
        [one, own, *arrived, Far(cotangent[0]), merge_weight, qkv_third, out_third, pack, patch],
        [Far((M_ROWS, M_COLS, C2)), slim, *strip_shapes, (M_PAD, A_ALL)],
        [((M_PAD, C2), F32), ((M_PAD, 3 * C2), BF16), ((M_PAD, C2), BF16), ((1, C2 // PAIR, 2 * M_PAD, M_PAD), BF16)],
    )
    acts_got = other_core(acts)
    arrived = send_strips((sa, sb, sd), -1)
    half_t = C2 // 2
    (grads_q,) = call(attention_grads, 4, [core], [acts, acts_got], [(64, 64, half_t)])
    part_q = scatter(grads_q, "x")
    own, sa, sb, sd, dqkv2, unit2, cot2 = call(
        second_back, 10, [],
        [Far(two_cot), *map(Far, arrived), Far(after(rolled, grads_q)), Far(qkv2), Far(p2), Far(qkv_second), Far(out_second), keep, place],
        [Far(slim), *map(Far, strip_shapes), Far(wide), Far(slim), Far(slim)], [(slim, BF16)], limit=56,
        order=(9, 10, 0, 1, 2, 3, 8, 4, 5, 6, 7),
    )
    arrived = send_strips((sa, sb, sd), 1)
    half = (64, 32, C1 // 2)
    keep2, send2 = call(block_grads, 4, [core], [Far(dqkv2), Far(unit2), Far(cot2), Far(o2)], [Far(half), Far(half)], limit=56)
    got2 = other_core(send2)
    piece = (16, 32, half_t)
    m = call(
        merge_grads, 4, [core, index("y")], [after(acts, own), acts_got], [piece] * 4, [((4, *piece), BF16)]
    )
    cot1, dqkv1, keep1, send1 = call(
        first_back, 9, [core], [Far(two_cot), Far(after(own, keep2, m[0])), *map(Far, arrived), Far(tok), Far(qkv1), Far(p1), Far(o1), Far(out_first), pack],
        [Far(slim), Far(wide), Far(half), Far(half)], [(slim, BF16), (slim, BF16)], limit=56,
        order=(10, 0, 1, 2, 3, 4, 9, 5, 6, 7, 8),
    )
    got1 = other_core(send1)
    m = onward(m, "y")
    (tokens_grad,) = call(first_input, 4, [], [cot1, dqkv1, Far(tok), qkv_first], [slim])
    (pairs,) = call(pack_pairs, 0.001, [], [keep2, got2, after(keep1, tokens_grad), got1], [(64, 64, C1 // 2)])
    q_piece, m_piece = (4, 64, half_t), (4, 32, half_t)
    parts = call(
        second_pieces, 3, [index(DEPTH), index("x")], [after(part_q.reshape(4, *q_piece), pairs), *m],
        [q_piece] * 4 + [m_piece] * 4, [((4, *m_piece), BF16)],
    )
    q, m = onward(parts[:4], DEPTH), onward(parts[4:], "x")
    swapped = to_chips(after(pairs, parts[0]))
    parts = call(
        last_pieces, 2, [index("y"), index(DEPTH)], [*q, *m], [q_piece[1:]] * 4 + [m_piece[1:]] * 4,
        [(q_piece, BF16), (m_piece, BF16)],
    )
    q, m = onward(parts[:4], "y"), onward(parts[4:], DEPTH)

    def halves(rows, width):
        return [jax.ShapeDtypeStruct((rows, width), F32), jax.ShapeDtypeStruct((rows, width), BF16)]

    total = [((32, 256), F32)]
    keep_s, send_s, keep_f, send_f = call(sums_block, 2, [core], [swapped], halves(16, 256) * 2, total)
    keep_t, send_t = call(sums_third, 0.001, [core], [*q, *m], halves(48, half_t))
    sizes = [(12, C1), (4, C1), (12, C1), (4, C1), (8, 2 * C2), (24, C2), (8, C2)]
    grads = call(
        finish, 2, [core],
        [keep_t, other_core(send_t), keep_s, other_core(send_s), keep_f, other_core(send_f)],
        [jax.ShapeDtypeStruct(s, F32) for s in sizes], [((16, 256), F32)],
    )
    return (latent[None], tokens_grad.reshape(tokens.shape), *grads)


def solution(mesh):
    split = Mesh(mesh.devices.reshape(4, 2, 2, 4, 2), EVERY)
    grid = P(None, LAT, LON, None)
    return jax.shard_map(
        on_device,
        mesh=split,
        in_specs=(grid,) + (P(),) * 7 + (grid,),
        out_specs=(grid, grid) + (P(EVERY, None),) * 7,
        check_vma=False,
    )
```

```python
import jax
import jax.numpy as jnp
import numpy as np
from jax import lax
from jax.experimental import pallas as pl
from jax.experimental.pallas import tpu as pltpu
from jax.sharding import Mesh, PartitionSpec as P

F32 = jnp.float32
BF16 = jnp.bfloat16
HDIM = 64
PAIR = 2 * HDIM
SCALE = HDIM ** (-0.5)
WA = 6
WO = 12
ROWS = 12
COLS = 24
TOK = ROWS * COLS
BAND = WA * COLS
C1 = 512
C2 = 1024
M_ROWS = 6
M_COLS = 12
M_TOK = M_ROWS * M_COLS
M_PAD = 80
STRIP_A = 64
STRIP_B = 64
STRIP_D = 32
STRIPS = STRIP_A + STRIP_B + STRIP_D
EPSILON = 1e-05
FAR = -1e30

NN = (((1,), (0,)), ((), ()))
NT = (((1,), (1,)), ((), ()))
TN = (((0,), (0,)), ((), ()))

LAT = ("x", "zh")
LON = ("zl", "y", "c")
DEPTH = ("zh", "zl")
CHIPS = ("x", "zh", "zl", "y")
EVERY = ("x", "zh", "zl", "y", "c")

A_CT = 0
A_O = A_CT + C2
A_DT = A_O + C2
A_N = A_DT + 3 * C2
A_HC = A_N + C2
A_NM = A_HC + C2
A_ALL = A_NM + 2 * C2


def routing():
    pack = np.zeros((STRIPS, TOK), np.float32)
    keep = np.zeros((TOK, TOK), np.float32)
    place = np.zeros((TOK, STRIPS), np.float32)
    half_a, half_o = WA // 2, WO // 2
    count = {"a": 0, "b": STRIP_A, "d": STRIP_A + STRIP_B}
    for r in range(ROWS):
        for c in range(COLS):
            gr, gc = r + half_a, c + half_o
            src = (gr % ROWS) * COLS + gc % COLS
            dst = r * COLS + c
            if gr < ROWS and gc < COLS:
                keep[dst, src] = 1
                continue
            kind = "a" if gc < COLS else ("b" if gr < ROWS else "d")
            slot = count[kind]
            count[kind] += 1
            pack[slot, src] = 1
            place[dst, slot] = 1
    patch = np.zeros((4 * M_PAD, TOK), np.float32)
    for part in range(4):
        for i in range(M_ROWS):
            for j in range(M_COLS):
                src = (2 * i + part % 2) * COLS + 2 * j + part // 2
                patch[part * M_PAD + i * M_COLS + j, src] = 1
    return [m.astype(jnp.bfloat16) for m in (pack, keep, place, patch)]


def dot(a, b, dims):
    return lax.dot_general(a, b, dims, preferred_element_type=F32)


def norm(field):
    values = field.astype(F32)
    centered = values - jnp.mean(values, axis=-1, keepdims=True)
    inverse = lax.rsqrt(jnp.mean(centered * centered, axis=-1, keepdims=True) + EPSILON)
    return centered * inverse, inverse


def norm_back(cotan, unit, inverse):
    cotan = cotan.astype(F32)
    along = jnp.mean(cotan * unit, axis=-1, keepdims=True)
    return (inverse * (cotan - jnp.mean(cotan, axis=-1, keepdims=True) - unit * along)).astype(BF16)


def add(a, b):
    return (a.astype(F32) + b.astype(F32)).astype(BF16)


def stacked(block):
    lane = lax.broadcasted_iota(jnp.int32, (1, PAIR), 1)
    first = jnp.where(lane < HDIM, 1.0, 0.0).astype(BF16)
    second = jnp.where(lane < HDIM, 0.0, 1.0).astype(BF16)
    return jnp.concatenate([block * first, block * second], axis=0)


def joined(both):
    size = both.shape[0] // 2
    lane = lax.broadcasted_iota(jnp.int32, (size, PAIR), 1)
    return jnp.where(lane < HDIM, both[:size], both[size:])


def softmax(queries, keys, bias):
    scores = dot(queries, keys, NT) * SCALE + bias
    raised = jnp.exp(scores - jnp.max(scores, axis=-1, keepdims=True))
    return raised * (1.0 / jnp.sum(raised, axis=-1, keepdims=True))


def attend(qkv_ref, o_ref, p_ref, channels, spans, biases):
    for n, ((start, size), bias) in enumerate(zip(spans, biases)):
        rows = pl.ds(start, size)
        for pair in range(channels // PAIR):
            lanes = pair * PAIR
            q = stacked(qkv_ref[rows, lanes : lanes + PAIR])
            k = qkv_ref[rows, channels + lanes : channels + lanes + PAIR]
            v = qkv_ref[rows, 2 * channels + lanes : 2 * channels + lanes + PAIR]
            p = softmax(q, k, bias).astype(BF16)
            p_ref[n, pair] = p
            o_ref[rows, lanes : lanes + PAIR] = joined(dot(p, v, NN)).astype(BF16)


def attend_back(qkv_ref, p_ref, do_ref, dqkv_ref, channels, spans):
    for n, (start, size) in enumerate(spans):
        rows = pl.ds(start, size)
        for pair in range(channels // PAIR):
            lanes = pair * PAIR
            q = stacked(qkv_ref[rows, lanes : lanes + PAIR])
            k = qkv_ref[rows, channels + lanes : channels + lanes + PAIR]
            v = qkv_ref[rows, 2 * channels + lanes : 2 * channels + lanes + PAIR]
            do = stacked(do_ref[rows, lanes : lanes + PAIR])
            p = p_ref[n, pair].astype(F32)
            dp = dot(do, v, NT)
            inner = jnp.sum(p * dp, axis=-1, keepdims=True)
            ds = (p * (dp - inner) * SCALE).astype(BF16)
            dq = joined(dot(ds, k, NN))
            dk = dot(ds, q, TN)
            dv = dot(p_ref[n, pair], do, TN)
            dqkv_ref[rows, lanes : lanes + PAIR] = dq.astype(BF16)
            dqkv_ref[rows, channels + lanes : channels + lanes + PAIR] = dk.astype(BF16)
            dqkv_ref[rows, 2 * channels + lanes : 2 * channels + lanes + PAIR] = dv.astype(BF16)


BANDS = [(0, BAND), (BAND, BAND)]


def band_biases(last_lat):
    def ids(dim, shape):
        token = lax.broadcasted_iota(jnp.int32, shape, dim)
        row = (token * 171) >> 12
        col = token - COLS * row
        return jnp.where(col >= WO, 1.0, 0.0), jnp.where(row >= WA // 2, 2.0, 0.0)

    win_q, half_q = ids(0, (BAND, BAND))
    win_k, half_k = ids(1, (BAND, BAND))
    plain = jnp.where(win_q == win_k, 0.0, FAR)
    plain = jnp.concatenate([plain, plain], axis=0)
    if last_lat is None:
        return [plain, plain]
    cut = jnp.where(win_q + half_q == win_k + half_k, 0.0, FAR)
    cut = jnp.concatenate([cut, cut], axis=0)
    return [plain, jnp.where(last_lat == 1, cut, plain)]


def put_strips(refs, strips):
    bounds = (0, STRIP_A, STRIP_A + STRIP_B, STRIPS)
    for ref, low, high in zip(refs, bounds[:-1], bounds[1:]):
        ref[...] = strips[low:high].astype(BF16)
        send(ref)


def send(*refs):
    for ref in refs:
        if isinstance(ref, Stored):
            ref.send()


def get_strips(refs):
    return jnp.concatenate([ref[...] for ref in refs], axis=0)


def first_forward(tok_ref, wqkv_ref, wo_ref, pack_ref, one_ref, out_a, out_b, out_d, qkv_ref, o_ref, p_ref):
    unit, _ = norm(tok_ref[...])
    qkv_ref[...] = dot(unit.astype(BF16), wqkv_ref[...], NT).astype(BF16)
    send(qkv_ref)
    attend(qkv_ref, o_ref, p_ref, C1, BANDS, band_biases(None))
    send(p_ref, o_ref)
    out = dot(o_ref[...], wo_ref[...], NT).astype(BF16)
    one = add(tok_ref[...], out)
    one_ref[...] = one
    put_strips((out_a, out_b, out_d), dot(pack_ref[...], one, NN))


def second_forward(
    last_ref, one_ref, in_a, in_b, in_d, wqkv_ref, wo_ref, keep_ref, place_ref,
    rolled_ref, own_ref, out_a, out_b, out_d, qkv_ref, o_ref, p_ref,
):
    arrived = get_strips((in_a, in_b, in_d))
    rolled = (dot(keep_ref[...], one_ref[...], NN) + dot(place_ref[...], arrived, NN)).astype(BF16)
    rolled_ref[...] = rolled
    unit, _ = norm(rolled)
    qkv_ref[...] = dot(unit.astype(BF16), wqkv_ref[...], NT).astype(BF16)
    send(qkv_ref, rolled_ref)
    attend(qkv_ref, o_ref, p_ref, C1, BANDS, band_biases(last_ref[0]))
    send(p_ref, o_ref)
    out = dot(o_ref[...], wo_ref[...], NT).astype(BF16)
    put_strips((out_a, out_b, out_d), dot(place_ref[...], out, TN))
    own_ref[...] = dot(keep_ref[...], out, TN).astype(BF16)


def third_both(
    one_ref, own_ref, in_a, in_b, in_d, ct_ref, wm_ref, wqkv_ref, wo_ref, pack_ref, patch_ref,
    latent_ref, two_cot_ref, out_a, out_b, out_d, acts_ref,
    wide, qkv_ref, do_ref, p_ref,
):
    arrived = get_strips((in_a, in_b, in_d))
    out_two = own_ref[...].astype(F32) + dot(pack_ref[...], arrived, TN)
    two = (one_ref[...].astype(F32) + out_two).astype(BF16)
    parts = dot(patch_ref[...], two, NN)
    merged = jnp.concatenate([parts[p * M_PAD : (p + 1) * M_PAD] for p in range(4)], axis=1)
    unit_m, inverse_m = norm(merged)
    acts_ref[:, A_NM : A_NM + 2 * C2] = unit_m.astype(BF16)
    hidden = dot(acts_ref[:, A_NM : A_NM + 2 * C2], wm_ref[...], NT).astype(BF16)
    unit_h, inverse_h = norm(hidden)
    acts_ref[:, A_N : A_N + C2] = unit_h.astype(BF16)
    qkv_ref[...] = dot(acts_ref[:, A_N : A_N + C2], wqkv_ref[...], NT).astype(BF16)
    key = lax.broadcasted_iota(jnp.int32, (2 * M_PAD, M_PAD), 1)
    bias = jnp.where(key < M_TOK, 0.0, FAR)
    span = [(0, M_PAD)]
    attend(qkv_ref, acts_ref.at[:, A_O : A_O + C2], p_ref, C2, span, [bias])
    out = dot(acts_ref[:, A_O : A_O + C2], wo_ref[...], NT).astype(BF16)
    wide[...] = hidden.astype(F32) + out.astype(F32)
    for i in range(M_ROWS):
        latent_ref[i] = wide[i * M_COLS : (i + 1) * M_COLS, :].astype(BF16)
    send(latent_ref)
    wide[M_TOK:, :] = jnp.zeros((M_PAD - M_TOK, C2), F32)
    for i in range(M_ROWS):
        wide[i * M_COLS : (i + 1) * M_COLS, :] = ct_ref[i].astype(F32)
    cot = wide[...].astype(BF16)
    acts_ref[:, A_CT : A_CT + C2] = cot
    do_ref[...] = dot(cot, wo_ref[...], NN).astype(BF16)
    attend_back(qkv_ref, p_ref, do_ref, acts_ref.at[:, A_DT : A_DT + 3 * C2], C2, span)
    dn = dot(acts_ref[:, A_DT : A_DT + 3 * C2], wqkv_ref[...], NN).astype(BF16)
    hidden_cot = add(cot, norm_back(dn, unit_h, inverse_h))
    acts_ref[:, A_HC : A_HC + C2] = hidden_cot
    send(acts_ref)
    dnm = dot(hidden_cot, wm_ref[...], NN).astype(BF16)
    merged_cot = norm_back(dnm, unit_m, inverse_m)
    two_cot = dot(patch_ref[0:M_PAD, :], merged_cot[:, 0:C1], TN)
    for p in range(1, 4):
        two_cot = two_cot + dot(
            patch_ref[p * M_PAD : (p + 1) * M_PAD, :], merged_cot[:, p * C1 : (p + 1) * C1], TN
        )
    two_cot = two_cot.astype(BF16)
    two_cot_ref[...] = two_cot
    send(two_cot_ref)
    put_strips((out_a, out_b, out_d), dot(pack_ref[...], two_cot, NN))


def both_cores(mine_ref, other_ref, start, width):
    where = pl.ds(start, width)
    return jnp.concatenate([mine_ref[:, where], other_ref[:, where]], axis=0)


def attention_grads(core_ref, mine_ref, other_ref, out_ref):
    half = C2 // 2
    n = both_cores(mine_ref, other_ref, pl.multiple_of(A_N + core_ref[0] * half, half), half)
    o = both_cores(mine_ref, other_ref, pl.multiple_of(A_O + core_ref[0] * half, half), half)
    for piece in range(8):
        step = 3 * C2 // 8
        grad = dot(both_cores(mine_ref, other_ref, A_DT + piece * step, step), n, TN).astype(BF16)
        out_ref[piece * 8 : piece * 8 + 8, 0:48] = grad.reshape(8, 48, half)
    for piece in range(4):
        step = C2 // 4
        grad = dot(both_cores(mine_ref, other_ref, A_CT + piece * step, step), o, TN).astype(BF16)
        out_ref[piece * 16 : piece * 16 + 16, 48:64] = grad.reshape(16, 16, half)


def merge_grads(core_ref, y_ref, mine_ref, other_ref, out_0, out_1, out_2, out_3, all_ref):
    half = C2 // 2
    nm = both_cores(mine_ref, other_ref, pl.multiple_of(A_NM + core_ref[0] * C2, C2), C2)
    for piece in range(4):
        step = C2 // 4
        hc = both_cores(mine_ref, other_ref, A_HC + piece * step, step)
        for side in range(2):
            grad = dot(hc, nm[:, side * half : side * half + half], TN).astype(BF16).reshape(4, 4, 16, half)
            for y in range(4):
                all_ref[y, piece * 4 : piece * 4 + 4, 16 * side : 16 * side + 16] = grad[:, y]
    for d, ref in enumerate((out_0, out_1, out_2, out_3)):
        ref[...] = all_ref[(y_ref[0] + d) % 4]


def sum_of(refs):
    total = refs[0][...].astype(F32)
    for ref in refs[1:]:
        total = total + ref[...].astype(F32)
    return total


def second_pieces(z_ref, x_ref, q_ref, m_0, m_1, m_2, m_3, q_out0, q_out1, q_out2, q_out3, o_0, o_1, o_2, o_3, m_ref):
    m_ref[...] = sum_of((m_0, m_1, m_2, m_3)).astype(BF16).reshape(4, 4, 32, C2 // 2)
    for d, (q, m) in enumerate(zip((q_out0, q_out1, q_out2, q_out3), (o_0, o_1, o_2, o_3))):
        q[...] = q_ref[(z_ref[0] + d) % 4]
        m[...] = m_ref[(x_ref[0] + d) % 4]


def last_pieces(
    y_ref, z_ref, q_0, q_1, q_2, q_3, m_0, m_1, m_2, m_3, p_0, p_1, p_2, p_3, o_0, o_1, o_2, o_3, q_ref, m_ref
):
    q_ref[...] = sum_of((q_0, q_1, q_2, q_3)).astype(BF16)
    m_ref[...] = sum_of((m_0, m_1, m_2, m_3)).astype(BF16)
    for d, (q, m) in enumerate(zip((p_0, p_1, p_2, p_3), (o_0, o_1, o_2, o_3))):
        q[...] = q_ref[(y_ref[0] + d) % 4]
        m[...] = m_ref[(z_ref[0] + d) % 4]


def pack_pairs(mine_s, other_s, mine_f, other_f, out_ref):
    out_ref[:, 0:32] = add(mine_s[...], other_s[...])
    out_ref[:, 32:64] = add(mine_f[...], other_f[...])


def block_grads(core_ref, dqkv_ref, unit_ref, cot_ref, o_ref, keep_out, send_out):
    half = C1 // 2
    for ref, side in ((send_out, 1 - core_ref[0]), (keep_out, core_ref[0])):
        where = pl.ds(pl.multiple_of(side * half, half), half)
        grad_qkv = dot(dqkv_ref[...], unit_ref[:, where], TN).reshape(64, 24, half)
        grad_out = dot(cot_ref[...], o_ref[:, where], TN).reshape(64, 8, half)
        ref[...] = jnp.concatenate([grad_qkv, grad_out], axis=1).astype(BF16)
        send(ref)


def second_back(
    two_cot_ref, in_a, in_b, in_d, rolled_ref, qkv_ref, p_ref, wqkv_ref, wo_ref, keep_ref, place_ref,
    own_ref, out_a, out_b, out_d, dqkv_ref, unit_ref, cot_ref,
    do_ref,
):
    unit, inverse = norm(rolled_ref[...])
    unit_ref[...] = unit.astype(BF16)
    arrived = get_strips((in_a, in_b, in_d))
    cot = (dot(keep_ref[...], two_cot_ref[...], NN) + dot(place_ref[...], arrived, NN)).astype(BF16)
    cot_ref[...] = cot
    do_ref[...] = dot(cot, wo_ref[...], NN).astype(BF16)
    attend_back(qkv_ref, p_ref, do_ref, dqkv_ref, C1, BANDS)
    send(unit_ref, cot_ref, dqkv_ref)
    dn = dot(dqkv_ref[...], wqkv_ref[...], NN).astype(BF16)
    rolled_cot = norm_back(dn, unit, inverse)
    put_strips((out_a, out_b, out_d), dot(place_ref[...], rolled_cot, TN))
    own_ref[...] = dot(keep_ref[...], rolled_cot, TN).astype(BF16)


def first_back(
    core_ref, two_cot_ref, own_ref, in_a, in_b, in_d, tok_ref, qkv_ref, p_ref, o_ref, wo_ref, pack_ref,
    cot_ref, dqkv_ref, grad_keep, grad_send,
    do_ref, unit_ref,
):
    unit_ref[...] = norm(tok_ref[...])[0].astype(BF16)
    arrived = get_strips((in_a, in_b, in_d))
    back = own_ref[...].astype(F32) + dot(pack_ref[...], arrived, TN)
    cot = (two_cot_ref[...].astype(F32) + back).astype(BF16)
    cot_ref[...] = cot
    do_ref[...] = dot(cot, wo_ref[...], NN).astype(BF16)
    attend_back(qkv_ref, p_ref, do_ref, dqkv_ref, C1, BANDS)
    send(cot_ref, dqkv_ref)
    block_grads(core_ref, dqkv_ref, unit_ref, cot_ref, o_ref, grad_keep, grad_send)


def first_input(cot_ref, dqkv_ref, tok_ref, wqkv_ref, grad_ref):
    unit, inverse = norm(tok_ref[...])
    dn = dot(dqkv_ref[...], wqkv_ref[...], NN).astype(BF16)
    grad_ref[...] = add(cot_ref[...], norm_back(dn, unit, inverse))


def split_cores(core, total, rows, at, keep_ref, send_ref, here):
    low, high = total[at : at + rows], total[at + rows : at + 2 * rows]
    keep_ref[here : here + rows] = jnp.where(core == 0, low, high)
    send_ref[here : here + rows] = jnp.where(core == 0, high, low).astype(BF16)


def sums_third(core_ref, q_0, q_1, q_2, q_3, m_0, m_1, m_2, m_3, keep_ref, send_ref):
    q, m = sum_of((q_0, q_1, q_2, q_3)), sum_of((m_0, m_1, m_2, m_3))
    split_cores(core_ref[0], q, 24, 0, keep_ref, send_ref, 0)
    split_cores(core_ref[0], q, 8, 48, keep_ref, send_ref, 24)
    for k in range(2):
        split_cores(core_ref[0], m, 8, 16 * k, keep_ref, send_ref, 32 + 8 * k)


def cut_block(core, total_ref, keep_ref, send_ref):
    for rows, at, here in ((12, 0, 0), (4, 24, 12)):
        low, high = total_ref[at : at + rows, :], total_ref[at + rows : at + 2 * rows, :]
        keep_ref[here : here + rows, :] = jnp.where(core == 0, low, high)
        send_ref[here : here + rows, :] = jnp.where(core == 0, high, low).astype(BF16)


def sums_block(core_ref, parts_ref, keep_s, send_s, keep_f, send_f, total_ref):
    total = parts_ref[0].astype(F32)
    for i in range(1, 64):
        total = total + parts_ref[i].astype(F32)
    for rows, keep_ref, send_ref in ((slice(0, 32), keep_s, send_s), (slice(32, 64), keep_f, send_f)):
        total_ref[...] = total[rows]
        cut_block(core_ref[0], total_ref, keep_ref, send_ref)


def finish(
    core_ref, keep_t, got_t, keep_s, got_s, keep_f, got_f,
    first_qkv, first_out, second_qkv, second_out, merge, third_qkv, third_out,
    wide_ref,
):
    core = core_ref[0]

    def place(ref, keep, got, col):
        width = keep.shape[1]
        for block, side in ((keep, core), (got, 1 - core)):
            start = pl.multiple_of(side * ref.shape[1] // 2 + col, 128)
            ref[:, pl.ds(start, width)] = block

    place(third_qkv, keep_t[0:24, :], got_t[0:24, :].astype(F32), 0)
    place(third_out, keep_t[24:32, :], got_t[24:32, :].astype(F32), 0)
    place(merge, keep_t[32:40, :], got_t[32:40, :].astype(F32), 0)
    place(merge, keep_t[40:48, :], got_t[40:48, :].astype(F32), C2 // 2)
    for keep, got, qkv, out in ((keep_s, got_s, second_qkv, second_out), (keep_f, got_f, first_qkv, first_out)):
        wide_ref[...] = got[...].astype(F32)
        place(qkv, keep[0:12, :], wide_ref[0:12, :], 0)
        place(out, keep[12:16, :], wide_ref[12:16, :], 0)


SMEM = pl.BlockSpec(memory_space=pltpu.SMEM)
VMEM = pl.BlockSpec(memory_space=pltpu.VMEM)
HBM = pl.BlockSpec(memory_space=pltpu.HBM)
ANY = pl.BlockSpec(memory_space=pl.ANY)


class Loaded:
    def __init__(self, far, near, semaphore):
        self.near, self.waited = near, False
        self.copy = pltpu.make_async_copy(far, near, semaphore)
        self.copy.start()

    def ready(self):
        if not self.waited:
            self.copy.wait()
            self.waited = True
        return self.near

    def __getitem__(self, where):
        return self.ready()[where]


class Stored:
    def __init__(self, far, near, semaphore):
        self.far, self.near, self.semaphore, self.copy = far, near, semaphore, None

    def send(self):
        if self.copy is None:
            self.copy = pltpu.make_async_copy(self.near, self.far, self.semaphore)
            self.copy.start()

    @property
    def shape(self):
        return self.near.shape

    @property
    def at(self):
        return self.near.at

    def __getitem__(self, where):
        return self.near[where]

    def __setitem__(self, where, value):
        self.near[where] = value


class Far:
    def __init__(self, what):
        self.what = what


def call(kernel, us, scalars, arrays, outs, scratch=(), limit=24, order=None):
    far_in = [isinstance(a, Far) for a in arrays]
    far_out = [isinstance(o, Far) for o in outs]
    arrays = [a.what if f else a for a, f in zip(arrays, far_in)]
    outs = [o.what if f else o for o, f in zip(outs, far_out)]
    outs = [o if isinstance(o, jax.ShapeDtypeStruct) else jax.ShapeDtypeStruct(o, BF16) for o in outs]
    staged_in = [a for a, f in zip(arrays, far_in) if f]
    staged_out = [o for o, f in zip(outs, far_out) if f]

    def body(*refs):
        refs = list(refs)
        take = lambda count: [refs.pop(0) for _ in range(count)]
        numbers, given, made = take(len(scalars)), take(len(arrays)), take(len(outs))
        near_in, near_out, own = take(len(staged_in)), take(len(staged_out)), take(len(scratch))
        in_sem, out_sem = refs
        count = 0
        slots = [i for i, far in enumerate(far_in) if far]
        for i in order or slots:
            count = slots.index(i)
            given[i] = Loaded(given[i], near_in[count], in_sem.at[count])
        count = 0
        for i, far in enumerate(far_out):
            if far:
                made[i] = Stored(made[i], near_out[count], out_sem.at[count])
                count += 1
        kernel(*numbers, *given, *made, *own)
        for ref in given:
            if isinstance(ref, Loaded):
                ref.ready()
        send(*made)
        for ref in made:
            if isinstance(ref, Stored):
                ref.copy.wait()

    return pl.pallas_call(
        body,
        name=kernel.__name__,
        out_shape=outs,
        in_specs=[SMEM] * len(scalars) + [HBM if f else VMEM for f in far_in],
        out_specs=[HBM if f else VMEM for f in far_out],
        scratch_shapes=[pltpu.VMEM(a.shape, a.dtype) for a in staged_in + staged_out]
        + [pltpu.VMEM(s, d) for s, d in scratch]
        + [pltpu.SemaphoreType.DMA((max(1, len(staged_in)),)), pltpu.SemaphoreType.DMA((max(1, len(staged_out)),))],
        cost_estimate=pl.CostEstimate(flops=int(us * 1.15e10), bytes_accessed=0, transcendentals=0),
        compiler_params=pltpu.CompilerParams(vmem_limit_bytes=limit * 2**20),
    )(*scalars, *arrays)


def after(block, *others):
    def nothing(*refs):
        pass

    return pl.pallas_call(
        nothing,
        cost_estimate=pl.CostEstimate(flops=1, bytes_accessed=0, transcendentals=0),
        name="after",
        out_shape=jax.ShapeDtypeStruct(block.shape, block.dtype),
        in_specs=[ANY] * (1 + len(others)),
        out_specs=ANY,
        input_output_aliases={0: 0},
    )(block, *others)


def send_strips(strips, step):
    lats, lons = 8, 16

    def route(lat_step, lon_step):
        return [
            (a * lons + o, (a + lat_step) % lats * lons + (o + lon_step) % lons)
            for a in range(lats)
            for o in range(lons)
        ]

    steps = ((step, 0), (0, step), (step, step))
    return [lax.ppermute(s, EVERY, route(*r)) for s, r in zip(strips, steps)]


def other_core(block):
    return lax.ppermute(block, "c", [(0, 1), (1, 0)])


def scatter(block, axis):
    return lax.psum_scatter(block, axis, scatter_dimension=0, tiled=True)


def to_chips(block):
    return lax.all_to_all(block, CHIPS, split_axis=0, concat_axis=0, tiled=True)


def onward(pieces, axis):
    moved = [
        lax.ppermute(piece, axis, [(i, (i + d) % 4) for i in range(4)])
        for d, piece in enumerate(pieces)
        if d > 0
    ]
    return [pieces[0], *moved]


def index(axes):
    return lax.axis_index(axes).astype(jnp.int32).reshape(1)


def on_device(
    tokens, qkv_first, out_first, qkv_second, out_second, merge_weight, qkv_third, out_third, cotangent
):
    pack, keep, place, patch = (Far(jnp.asarray(m)) for m in routing())
    core = index("c")
    last = (index(LAT) == 7).astype(jnp.int32)
    tok = tokens.reshape(TOK, C1)
    wide, slim = (TOK, 3 * C1), (TOK, C1)
    strip_shapes = [(STRIP_A, C1), (STRIP_B, C1), (STRIP_D, C1)]
    probs = (2, C1 // PAIR, 2 * BAND, BAND)
    one, sa, sb, sd, qkv1, o1, p1 = call(
        first_forward, 5, [], [Far(tok), Far(qkv_first), Far(out_first), pack],
        [Far(slim), *map(Far, strip_shapes), Far(wide), Far(slim), Far(probs)], limit=56,
    )
    arrived = send_strips((sa, sb, sd), -1)
    rolled, own, sa, sb, sd, qkv2, o2, p2 = call(
        second_forward, 6, [last], [Far(one), *map(Far, arrived), Far(qkv_second), Far(out_second), keep, place],
        [Far(slim), Far(slim), *map(Far, strip_shapes), Far(wide), Far(slim), Far(probs)], limit=40,
        order=(6, 7, 0, 1, 2, 3, 4, 5),
    )
    arrived = send_strips((sa, sb, sd), 1)
    latent, two_cot, sa, sb, sd, acts = call(
        third_both, 18, [],
        [one, own, *arrived, Far(cotangent[0]), merge_weight, qkv_third, out_third, pack, patch],
        [Far((M_ROWS, M_COLS, C2)), slim, *strip_shapes, (M_PAD, A_ALL)],
        [((M_PAD, C2), F32), ((M_PAD, 3 * C2), BF16), ((M_PAD, C2), BF16), ((1, C2 // PAIR, 2 * M_PAD, M_PAD), BF16)],
    )
    acts_got = other_core(acts)
    arrived = send_strips((sa, sb, sd), -1)
    half_t = C2 // 2
    (grads_q,) = call(attention_grads, 4, [core], [acts, acts_got], [(64, 64, half_t)])
    part_q = scatter(grads_q, "x")
    own, sa, sb, sd, dqkv2, unit2, cot2 = call(
        second_back, 10, [],
        [Far(two_cot), *map(Far, arrived), Far(after(rolled, grads_q)), Far(qkv2), Far(p2), Far(qkv_second), Far(out_second), keep, place],
        [Far(slim), *map(Far, strip_shapes), Far(wide), Far(slim), Far(slim)], [(slim, BF16)], limit=56,
        order=(4, 9, 10, 0, 1, 2, 3, 8, 5, 6, 7),
    )
    arrived = send_strips((sa, sb, sd), 1)
    half = (64, 32, C1 // 2)
    keep2, send2 = call(block_grads, 4, [core], [Far(dqkv2), Far(unit2), Far(cot2), Far(o2)], [Far(half), Far(half)], limit=56)
    got2 = other_core(send2)
    piece = (16, 32, half_t)
    m = call(
        merge_grads, 4, [core, index("y")], [after(acts, own), acts_got], [piece] * 4, [((4, *piece), BF16)]
    )
    cot1, dqkv1, keep1, send1 = call(
        first_back, 9, [core], [Far(two_cot), Far(after(own, keep2, m[0])), *map(Far, arrived), Far(tok), Far(qkv1), Far(p1), Far(o1), Far(out_first), pack],
        [Far(slim), Far(wide), Far(half), Far(half)], [(slim, BF16), (slim, BF16)], limit=56,
        order=(5, 10, 0, 1, 2, 3, 4, 9, 6, 7, 8),
    )
    got1 = other_core(send1)
    m = onward(m, "y")
    (tokens_grad,) = call(first_input, 4, [], [cot1, dqkv1, Far(tok), qkv_first], [slim])
    (pairs,) = call(pack_pairs, 0.001, [], [keep2, got2, after(keep1, tokens_grad), got1], [(64, 64, C1 // 2)])
    q_piece, m_piece = (4, 64, half_t), (4, 32, half_t)
    parts = call(
        second_pieces, 3, [index(DEPTH), index("x")], [after(part_q.reshape(4, *q_piece), pairs), *m],
        [q_piece] * 4 + [m_piece] * 4, [((4, *m_piece), BF16)],
    )
    q, m = onward(parts[:4], DEPTH), onward(parts[4:], "x")
    swapped = to_chips(after(pairs, parts[0]))
    parts = call(
        last_pieces, 2, [index("y"), index(DEPTH)], [*q, *m], [q_piece[1:]] * 4 + [m_piece[1:]] * 4,
        [(q_piece, BF16), (m_piece, BF16)],
    )
    q, m = onward(parts[:4], "y"), onward(parts[4:], DEPTH)

    def halves(rows, width):
        return [jax.ShapeDtypeStruct((rows, width), F32), jax.ShapeDtypeStruct((rows, width), BF16)]

    total = [((32, 256), F32)]
    keep_s, send_s, keep_f, send_f = call(sums_block, 2, [core], [swapped], halves(16, 256) * 2, total)
    keep_t, send_t = call(sums_third, 0.001, [core], [*q, *m], halves(48, half_t))
    sizes = [(12, C1), (4, C1), (12, C1), (4, C1), (8, 2 * C2), (24, C2), (8, C2)]
    grads = call(
        finish, 2, [core],
        [keep_t, other_core(send_t), keep_s, other_core(send_s), keep_f, other_core(send_f)],
        [jax.ShapeDtypeStruct(s, F32) for s in sizes], [((16, 256), F32)],
    )
    return (latent[None], tokens_grad.reshape(tokens.shape), *grads)


def solution(mesh):
    split = Mesh(mesh.devices.reshape(4, 2, 2, 4, 2), EVERY)
    grid = P(None, LAT, LON, None)
    return jax.shard_map(
        on_device,
        mesh=split,
        in_specs=(grid,) + (P(),) * 7 + (grid,),
        out_specs=(grid, grid) + (P(EVERY, None),) * 7,
        check_vma=False,
    )
```
